512 devices in a mesh: ctx: 32 (over z, x), ch: 16 (over y, core).
Axes of the slice: x: 4, y: 8, z: 8, core: 2. Of those that a mesh axis runs over, the one named last changes fastest.
Arguments:
- gate_outer: bfloat16 [4096, 4096], P('ctx', 'ch'), may hold values from -70 to 70
- gate_inner: bfloat16 [4096, 4096], P('ctx', 'ch'), may hold values from -6 to 6
- conv_input: bfloat16 [4096, 4096], P('ctx', 'ch'), may hold values from -6 to 6
- filters: bfloat16 [256, 128], P('ch'), may hold values from -0.5 to 0.5
- queries: bfloat16 [4096, 4096], P('ctx', 'ch'), may hold values from -5.5 to 5.5
- keys: bfloat16 [4096, 4096], P('ctx', 'ch'), may hold values from -5.5 to 5.5
- cotangent: bfloat16 [4096, 4096], P('ctx', 'ch'), may hold values from -6 to 6
Outputs:
- attended: bfloat16 [4096, 4096], P('ctx', 'ch')
- grad_query: bfloat16 [4096, 4096], P('ctx', 'ch')
- grad_key: bfloat16 [4096, 4096], P('ctx', 'ch')
- grad_gate_outer: bfloat16 [4096, 4096], P('ctx', 'ch')
- grad_filters: float32 [256, 128], P('ch')
The draws below stay inside these ranges and needn't reach their ends.
All inputs are finite; a program needn't handle non-finite values.
Results may differ from the reference program's by a relative error of at most 0.012.
The reference program's roundings to bfloat16 on the way count: a program that leaves them out, or rounds other values in their place, can miss the bound.
Values may be sent and summed in bfloat16 or wider, within the bound.
A program may use at most 64 MiB of HBM per device.

```python
import math
import jax
import jax.numpy as jnp
from jax import lax

HEAD_DIM = 128
TAPS = 128
SEQ = 4096
CHANNELS = 4096
FILTERS = 256


def scaled_rows(key, length, breadth, trend_rate):
    first_key, second_key, third_key = jax.random.split(key, 3)
    row_scale = jnp.exp(jax.random.uniform(first_key, (length, 1), jnp.float32, -1.15, 1.15))
    col_scale = jnp.exp(jax.random.uniform(second_key, (1, breadth), jnp.float32, -1.15, 1.15))
    col_slope = jnp.exp(trend_rate * jnp.arange(breadth, dtype=jnp.float32)[None, :] / breadth)
    return (row_scale * col_scale * col_slope, third_key)


def draw_gate_outer(key, part):
    key = jax.random.fold_in(key, 5)
    factors, inner_key = scaled_rows(key, SEQ, CHANNELS, 0.55)
    base_draw = jnp.clip(jax.random.normal(inner_key, (SEQ, CHANNELS), jnp.float32), -4.0, 4.0)
    return (factors * base_draw).astype(jnp.bfloat16)


def draw_queries(key, part):
    key = jax.random.fold_in(key, 7)
    base_draw = 1.7 * jnp.clip(jax.random.normal(key, (SEQ, CHANNELS), jnp.float32), -3.2, 3.2)
    return base_draw.astype(jnp.bfloat16)


def draw_keys(key, part):
    key = jax.random.fold_in(key, 9)
    base_draw = 1.7 * jnp.clip(jax.random.normal(key, (SEQ, CHANNELS), jnp.float32), -3.2, 3.2)
    return base_draw.astype(jnp.bfloat16)


def block_levels(rng, dims, cuts, low, top_value):
    gain = 1.0
    for position, blocks in cuts:
        steps = jax.random.uniform(jax.random.fold_in(jax.random.fold_in(rng, 6), position), (blocks,), jnp.float32, low / len(cuts), top_value / len(cuts))
        gain = gain * jnp.repeat(jnp.exp(steps), dims[position] // blocks).reshape((-1,) + (1,) * (len(dims) - 1 - position))
    return gain


def centred(rng, extent, width, bound, shards=(), held_as=jnp.bfloat16):
    level = block_levels(rng, extent, shards, -0.22, 0.18) if shards else 1.0
    values = jax.random.normal(rng, extent, jnp.float32) * width * level
    return jnp.minimum(jnp.maximum(values, -bound), bound).astype(held_as)


def setup_inputs(seed: int = 0) -> dict:
    splits = jax.random.split(jax.random.key(seed), 8)
    return {
        "gate_outer": draw_gate_outer(jax.random.fold_in(splits[7], 71), 0),
        "gate_inner": centred(splits[1], (SEQ, CHANNELS), 1.0, 6.0, ((0, 32), (1, 16))),
        "conv_input": centred(splits[2], (SEQ, CHANNELS), 1.0, 6.0, ((0, 32), (1, 16))),
        "filters": centred(splits[3], (FILTERS, TAPS), TAPS ** -0.5, 0.5, ((0, 16),)),
        "queries": draw_queries(jax.random.fold_in(splits[7], 71), 0),
        "keys": draw_keys(jax.random.fold_in(splits[7], 71), 0),
        "cotangent": centred(splits[6], (SEQ, CHANNELS), 1.0, 6.0, ((0, 32), (1, 16))),
    }


NEGATIVE = -1e+30
EPSILON = 1e-05

def to_heads(matrix):
    return matrix.reshape(matrix.shape[0], -1, HEAD_DIM).transpose(1, 0, 2)

def from_heads(stacked):
    return stacked.transpose(1, 0, 2).reshape(stacked.shape[1], -1)

def head_pass(operands):
    query_rows, key_rows, value_rows, cot_rows = operands
    score_scale = 1.0 / math.sqrt(HEAD_DIM)
    seq_length = query_rows.shape[0]
    place_id = jnp.arange(seq_length, dtype=jnp.int32)
    allowed = place_id[:, None] >= place_id[None, :]
    scores = jnp.dot(query_rows, key_rows.T, preferred_element_type=jnp.float32) * score_scale
    masked = jnp.where(allowed, scores, NEGATIVE)
    row_top = lax.optimization_barrier(jnp.max(masked, axis=1))
    log_total = row_top + jnp.log(lax.optimization_barrier(jnp.sum(jnp.where(allowed, jnp.exp(masked - row_top[:, None]), 0.0), axis=1)))
    weights = jnp.where(allowed, jnp.exp(masked - log_total[:, None]), 0.0)
    prob_low = weights.astype(jnp.bfloat16)
    attended = jnp.dot(prob_low, value_rows, preferred_element_type=jnp.float32).astype(jnp.bfloat16)
    attended_wide = lax.optimization_barrier(attended).astype(jnp.float32)
    row_delta = lax.optimization_barrier(jnp.sum(cot_rows.astype(jnp.float32) * attended_wide, axis=1))
    prob_grad = jnp.dot(cot_rows, value_rows.T, preferred_element_type=jnp.float32)
    score_grad = (weights * (prob_grad - row_delta[:, None])).astype(jnp.bfloat16)
    grad_query = (jnp.dot(score_grad, key_rows, preferred_element_type=jnp.float32) * score_scale).astype(jnp.bfloat16)
    grad_key = (jnp.dot(score_grad.T, query_rows, preferred_element_type=jnp.float32) * score_scale).astype(jnp.bfloat16)
    grad_values = jnp.dot(prob_low.T, cot_rows, preferred_element_type=jnp.float32)
    return (attended, grad_query, grad_key, grad_values)

def reference(gate_outer, gate_inner, conv_input, filters, queries, keys, cotangent):
    seq_length, chan_count = gate_outer.shape
    tap_count = filters.shape[1]
    group_size = chan_count // filters.shape[0]
    product = (gate_inner.astype(jnp.float32) * conv_input.astype(jnp.float32)).astype(jnp.bfloat16)
    product_wide = lax.optimization_barrier(product).astype(jnp.float32)
    padded = jnp.concatenate([jnp.zeros((tap_count - 1, chan_count), jnp.float32), product_wide], axis=0)
    expanded = jnp.repeat(filters.astype(jnp.float32), group_size, axis=0)

    def add_tap(tap_index, running):
        shifted = lax.dynamic_slice_in_dim(padded, tap_count - 1 - tap_index, seq_length, 0)
        column = lax.dynamic_slice_in_dim(expanded, tap_index, 1, 1)
        return running + column[:, 0][None, :] * shifted
    conv_out = lax.fori_loop(0, tap_count, add_tap, jnp.zeros((seq_length, chan_count), jnp.float32))
    mixer = gate_outer.astype(jnp.float32) * conv_out
    inv_rms = lax.rsqrt(lax.optimization_barrier(jnp.sum(mixer * mixer, axis=1)) / chan_count + EPSILON)
    values = (mixer * inv_rms[:, None]).astype(jnp.bfloat16)
    attended, grad_query, grad_key, grad_values = lax.map(head_pass, (to_heads(queries), to_heads(keys), to_heads(values), to_heads(cotangent)))
    grad_values = from_heads(grad_values)
    projection = lax.optimization_barrier(jnp.sum(grad_values * mixer, axis=1))
    cube = inv_rms * inv_rms * inv_rms
    mixer_grad = inv_rms[:, None] * grad_values - mixer * (cube * projection / chan_count)[:, None]
    grad_gate_outer = (mixer_grad * conv_out).astype(jnp.bfloat16)
    conv_low = (mixer_grad * gate_outer.astype(jnp.float32)).astype(jnp.bfloat16)
    conv_grad = lax.optimization_barrier(conv_low).astype(jnp.float32)

    def tap_grad(tap_index):
        shifted = lax.dynamic_slice_in_dim(padded, tap_count - 1 - tap_index, seq_length, 0)
        return lax.optimization_barrier(jnp.sum(conv_grad * shifted, axis=0)).reshape(-1, group_size).sum(axis=1)
    grad_filters = lax.map(tap_grad, jnp.arange(tap_count, dtype=jnp.int32)).T
    return (from_heads(attended), from_heads(grad_query), from_heads(grad_key), grad_gate_outer, grad_filters)
```

```python
import functools
import math

import jax
import jax.numpy as jnp
from jax import lax
from jax.experimental import pallas as pl
from jax.experimental.pallas import tpu as pltpu
from jax.sharding import PartitionSpec as P

MESH = pl.DeviceIdType.MESH
HEAD_DIM = 128
NEGATIVE = -1e30
EPSILON = 1e-05
NX = 4
NC = 2
F32 = jnp.float32
BF16 = jnp.bfloat16

NT = (((1,), (1,)), ((), ()))
NN = (((1,), (0,)), ((), ()))
TN = (((0,), (0,)), ((), ()))


def dot(a, b, dims):
    return lax.dot_general(a, b, dims, preferred_element_type=F32)


def kernel(
    NZ, NY,
    go, gi, ci, filt, q, k, cot,
    att_o, dq_o, dk_o, ggo_o, gf_o,
    k_all, v_all, q_all, c_all, win, toep, s_buf, dp_buf, p_low, ds_low,
    lse_buf, d_buf, core_buf, y_buf, fx_buf, fz_buf,
    dv_src, dv_buf, dk_src, dk_buf, att_src, att_buf, dq_src, dq_buf,
    mix_buf, conv_buf, win_back, lse_sum, delta_sum,
    ssem, rk, rv, rq, rc, rhalo, rlse, rd, rcore, ry, rdv, rdk, ratt, rdq, rfx, rfz,
):
    rows, chans = go.shape
    groups, taps = filt.shape
    group_size = chans // groups
    heads = chans // HEAD_DIM
    width = chans * NY * NC
    scale = 1.0 / math.sqrt(HEAD_DIM)
    ctx, ch = lax.axis_index("ctx"), lax.axis_index("ch")
    z, x = ctx // NX, ctx % NX
    y, core = ch // NC, ch % NC
    last = NZ * NX - 1

    def z_dev(zp):
        return (zp * NX + x, ch)

    def x_dev(xp):
        return (z * NX + xp, ch)

    def y_dev(yp):
        return (ctx, yp * NC + core)

    sibling = (ctx, y * NC + (1 - core))
    z_peer = [lax.rem(z + o, NZ) for o in range(NZ)]
    x_peer = [lax.rem(x + o, NX) for o in range(NX)]
    y_peer = [lax.rem(y + o, NY) for o in range(NY)]
    near = lambda n: [o for d in range(1, n // 2 + 1) for o in dict.fromkeys((d, n - d))]
    z_order, x_order, y_order = near(NZ), near(NX), near(NY)
    before = lax.rem(ctx + last, last + 1)
    after = lax.rem(ctx + 1, last + 1)

    sends = []

    def push(src, dst, recv_sem, dev):
        copy = pltpu.make_async_remote_copy(
            src_ref=src, dst_ref=dst, send_sem=ssem.at[len(sends)], recv_sem=recv_sem,
            device_id=dev, device_id_type=MESH,
        )
        sends.append(copy)
        copy.start()

    def arrive(dst, recv_sem, dev):
        pltpu.make_async_remote_copy(
            src_ref=dst, dst_ref=dst, send_sem=ssem.at[0], recv_sem=recv_sem,
            device_id=dev, device_id_type=MESH,
        ).wait_recv()

    barrier = pltpu.get_barrier_semaphore()
    greeted = 0
    for dev in (
        [z_dev(z_peer[o]) for o in z_order]
        + [x_dev(x_peer[o]) for o in x_order]
        + [y_dev(y_peer[o]) for o in y_order]
        + [sibling, (before, ch)]
    ):
        pl.semaphore_signal(barrier, inc=1, device_id=dev, device_id_type=MESH)
        greeted += 1

    x_rows = pl.ds(pl.multiple_of(x * rows, rows), rows)
    k_all[x_rows] = k[...]
    q_all[z] = q[...]
    c_all[z] = cot[...]
    win[rows:] = (gi[...].astype(F32) * ci[...].astype(F32)).astype(BF16)
    flip = (
        lax.broadcasted_iota(jnp.int32, (taps, 2 * taps), 0)
        + lax.broadcasted_iota(jnp.int32, (taps, 2 * taps), 1)
        == taps
    ).astype(F32).astype(BF16)
    turned = dot(filt[...], flip, NN)
    for g in range(groups):
        spread = jnp.broadcast_to(turned[g : g + 1], (rows, 2 * taps))
        spread = pltpu.roll(spread, 0, 1, stride=1, stride_axis=0)
        toep[g * rows : (g + 1) * rows] = spread.astype(BF16)

    pl.semaphore_wait(barrier, greeted)

    @pl.when(ctx < last)
    def _():
        pltpu.make_async_remote_copy(
            src_ref=win.at[pl.ds(rows, rows)], dst_ref=win.at[pl.ds(0, rows)],
            send_sem=ssem.at[ssem.shape[0] - 1], recv_sem=rhalo,
            device_id=(after, ch), device_id_type=MESH,
        ).start()

    for o in x_order:
        push(k, k_all.at[x_rows], rk.at[x], x_dev(x_peer[o]))
    for o in z_order:
        push(q, q_all.at[z], rq.at[z], z_dev(z_peer[o]))
    for o in z_order:
        push(cot, c_all.at[z], rc.at[z], z_dev(z_peer[o]))

    @pl.when(ctx > 0)
    def _():
        pltpu.make_async_remote_copy(
            src_ref=win.at[pl.ds(0, rows)], dst_ref=win.at[pl.ds(0, rows)],
            send_sem=ssem.at[0], recv_sem=rhalo, device_id=(before, ch), device_id_type=MESH,
        ).wait_recv()

    @pl.when(ctx == 0)
    def _():
        win[:rows] = jnp.zeros((rows, chans), BF16)

    lane_group = lax.broadcasted_iota(jnp.int32, (rows, chans), 1) // group_size
    window = win[...]
    conv = jnp.zeros((rows, chans), F32)
    for g in range(groups):
        part = dot(toep[g * rows : (g + 1) * rows], window, NN)
        conv = jnp.where(lane_group == g, part, conv)
    conv_buf[...] = conv
    back = (
        lax.broadcasted_iota(jnp.int32, (2 * rows, 2 * rows), 0)
        + lax.broadcasted_iota(jnp.int32, (2 * rows, 2 * rows), 1)
        == 2 * rows - 1
    ).astype(F32).astype(BF16)
    win_back[...] = dot(back, window, NN).astype(BF16)
    mixer = go[...].astype(F32) * conv
    mix_buf[...] = mixer

    def as_row(column):
        return jnp.broadcast_to(column, (rows, 128)).T[:8]

    def as_tile(row):
        tile = jnp.broadcast_to(row[0:1], (128, rows)).T
        return jnp.concatenate([tile] * (chans // 128), axis=1)

    def to_sibling(phase, column):
        core_buf[phase, core] = as_row(column)
        push(core_buf.at[phase, core], core_buf.at[phase, core], rcore.at[phase], sibling)

    def to_y(phase):
        arrive(core_buf.at[phase, 1 - core], rcore.at[phase], sibling)
        y_buf[phase, y] = core_buf[phase, 0] + core_buf[phase, 1]
        for o in y_order:
            push(y_buf.at[phase, y], y_buf.at[phase, y], ry.at[phase, y], y_dev(y_peer[o]))

    def from_y(phase):
        for o in y_order:
            arrive(y_buf.at[phase, y_peer[o]], ry.at[phase, y_peer[o]], y_dev(y_peer[o]))
        total = y_buf[phase, 0]
        for i in range(1, NY):
            total = total + y_buf[phase, i]
        return as_tile(total)

    to_sibling(0, jnp.sum(mixer * mixer, axis=1, keepdims=True))
    to_y(0)

    keys = NX * rows
    ahead = lax.broadcasted_iota(jnp.int32, (keys, rows), 1) - lax.broadcasted_iota(
        jnp.int32, (keys, rows), 0
    )

    def z_at(i):
        step = jnp.where(i % 2 == 1, (i + 1) // 2, NZ - i // 2)
        return lax.rem(z + step, NZ)

    def score_block(zp):
        allowed = ahead >= (z - zp) * keys - x * rows
        for h in range(heads):
            cols = slice(h * HEAD_DIM, (h + 1) * HEAD_DIM)
            scores = dot(k_all[:, cols], q_all[zp, :, cols], NT) * scale
            scores = jnp.where(allowed, scores, NEGATIVE)
            top = jnp.max(scores, axis=0, keepdims=True)
            total = jnp.sum(jnp.exp(scores - top), axis=0, keepdims=True)
            s_buf[zp * heads + h] = scores
            lse_buf[z, pl.ds(zp * heads + h, 1), :] = top + jnp.log(total)

    def score_step(i, carry):
        zp = z_at(i)
        arrive(q_all.at[zp], rq.at[zp], z_dev(zp))
        score_block(zp)
        return carry

    for o in x_order:
        xp = x_peer[o]
        arrive(k_all.at[pl.ds(pl.multiple_of(xp * rows, rows), rows)], rk.at[xp], x_dev(xp))
    score_block(z)
    split = min(3, NZ)
    lax.fori_loop(1, split, score_step, 0)

    inv = lax.rsqrt(from_y(0) / width + EPSILON)
    v_all[x_rows] = (mix_buf[...] * inv).astype(BF16)
    for o in x_order:
        push(v_all.at[x_rows], v_all.at[x_rows], rv.at[x], x_dev(x_peer[o]))

    lax.fori_loop(split, NZ, score_step, 0)
    for o in z_order:
        push(lse_buf.at[z], lse_buf.at[z], rlse.at[z], z_dev(z_peer[o]))

    for o in x_order:
        xp = x_peer[o]
        arrive(v_all.at[pl.ds(pl.multiple_of(xp * rows, rows), rows)], rv.at[xp], x_dev(xp))

    def dprob_block(zp):
        for h in range(heads):
            cols = slice(h * HEAD_DIM, (h + 1) * HEAD_DIM)
            dp_buf[zp * heads + h] = dot(v_all[:, cols], c_all[zp, :, cols], NT)

    def dprob_step(i, carry):
        zp = z_at(i)
        arrive(c_all.at[zp], rc.at[zp], z_dev(zp))
        dprob_block(zp)
        return carry

    dprob_block(z)
    lax.fori_loop(1, NZ, dprob_step, 0)

    for o in z_order:
        zp = z_peer[o]
        arrive(lse_buf.at[zp], rlse.at[zp], z_dev(zp))
    parts = lse_buf[...]
    top = jnp.max(parts, axis=0)
    lse_sum[...] = top + jnp.log(jnp.sum(jnp.exp(parts - top[None]), axis=0))

    def prob_block(zp, carry):
        for h in range(heads):
            row = zp * heads + h
            weights = jnp.exp(s_buf[row] - lse_sum[pl.ds(row, 1), :])
            s_buf[row] = weights
            p_low[h, :, pl.ds(pl.multiple_of(zp * rows, rows), rows)] = weights.astype(BF16)
            d_buf[z, pl.ds(row, 1), :] = jnp.sum(weights * dp_buf[row], axis=0, keepdims=True)
        return carry

    lax.fori_loop(0, NZ, prob_block, 0)
    for o in z_order:
        push(d_buf.at[z], d_buf.at[z], rd.at[z], z_dev(z_peer[o]))

    def columns(ref, h):
        cols = slice(h * HEAD_DIM, (h + 1) * HEAD_DIM)
        return ref[:, :, cols].reshape(NZ * rows, HEAD_DIM)

    for h in range(heads):
        cols = slice(h * HEAD_DIM, (h + 1) * HEAD_DIM)
        dv_src[:, cols] = dot(p_low[h], columns(c_all, h), NN).astype(BF16)
    for o in x_order:
        xp = x_peer[o]
        push(dv_src.at[pl.ds(pl.multiple_of(xp * rows, rows), rows)], dv_buf.at[x], rdv.at[x], x_dev(xp))
    dv_buf[x] = dv_src[x_rows]

    def across(src, low, ref):
        for h in range(heads):
            cols = slice(h * HEAD_DIM, (h + 1) * HEAD_DIM)
            full = dot(ref[:, cols], low[h], TN).astype(BF16)
            for i in range(NZ):
                src[i, cols, :] = full[:, i * rows : (i + 1) * rows]

    across(att_src, p_low, v_all)
    for o in z_order:
        zp = z_peer[o]
        push(att_src.at[zp], att_buf.at[z], ratt.at[z], z_dev(zp))
    att_buf[z] = att_src[z]

    for o in x_order:
        xp = x_peer[o]
        arrive(dv_buf.at[xp], rdv.at[xp], x_dev(xp))
    value_grad = dv_buf[0].astype(F32)
    for i in range(1, NX):
        value_grad = value_grad + dv_buf[i].astype(F32)
    to_sibling(1, jnp.sum(value_grad * mix_buf[...], axis=1, keepdims=True))
    to_y(1)

    for o in z_order:
        zp = z_peer[o]
        arrive(d_buf.at[zp], rd.at[zp], z_dev(zp))
    delta = d_buf[0]
    for i in range(1, NZ):
        delta = delta + d_buf[i]
    delta_sum[...] = delta

    def dscore_block(zp, carry):
        for h in range(heads):
            row = zp * heads + h
            dscore = s_buf[row] * (dp_buf[row] - delta_sum[pl.ds(row, 1), :])
            ds_low[h, :, pl.ds(pl.multiple_of(zp * rows, rows), rows)] = dscore.astype(BF16)
        return carry

    lax.fori_loop(0, NZ, dscore_block, 0)
    across(dq_src, ds_low, k_all)
    for o in z_order:
        zp = z_peer[o]
        push(dq_src.at[zp], dq_buf.at[z], rdq.at[z], z_dev(zp))
    dq_buf[z] = dq_src[z]
    for h in range(heads):
        cols = slice(h * HEAD_DIM, (h + 1) * HEAD_DIM)
        dk_src[:, cols] = dot(ds_low[h], columns(q_all, h), NN).astype(BF16)
    for o in x_order:
        xp = x_peer[o]
        push(dk_src.at[pl.ds(pl.multiple_of(xp * rows, rows), rows)], dk_buf.at[x], rdk.at[x], x_dev(xp))
    dk_buf[x] = dk_src[x_rows]

    proj = from_y(1)
    mixer_grad = inv * value_grad - mix_buf[...] * (inv * inv * inv * proj / width)
    ggo_o[...] = (mixer_grad * conv_buf[...]).astype(BF16)
    conv_grad = (mixer_grad * go[...].astype(F32)).astype(BF16)
    sums = []
    for g in range(groups):
        pairs = dot(jnp.where(lane_group == g, conv_grad.astype(F32), 0.0).astype(BF16), win_back[...], NT)
        pairs = pltpu.roll(pairs, 1, 1, stride=1, stride_axis=0)
        sums.append(jnp.sum(pairs[:, taps:], axis=0, keepdims=True))
    fx_buf[x] = jnp.concatenate(sums, axis=0)
    for o in x_order:
        push(fx_buf.at[x], fx_buf.at[x], rfx.at[x], x_dev(x_peer[o]))
    for o in x_order:
        xp = x_peer[o]
        arrive(fx_buf.at[xp], rfx.at[xp], x_dev(xp))
    total = fx_buf[0]
    for i in range(1, NX):
        total = total + fx_buf[i]
    fz_buf[z] = total
    for o in z_order:
        push(fz_buf.at[z], fz_buf.at[z], rfz.at[z], z_dev(z_peer[o]))

    def from_z(buf, sem, factor, out):
        for o in z_order:
            zp = z_peer[o]
            arrive(buf.at[zp], sem.at[zp], z_dev(zp))
        total = buf[0].astype(F32)
        for i in range(1, NZ):
            total = total + buf[i].astype(F32)
        for h in range(heads):
            cols = slice(h * HEAD_DIM, (h + 1) * HEAD_DIM)
            out[:, cols] = (total[cols].T * factor).astype(BF16)

    from_z(att_buf, ratt, 1.0, att_o)
    for o in x_order:
        xp = x_peer[o]
        arrive(dk_buf.at[xp], rdk.at[xp], x_dev(xp))
    key_grad = dk_buf[0].astype(F32)
    for i in range(1, NX):
        key_grad = key_grad + dk_buf[i].astype(F32)
    dk_o[...] = (key_grad * scale).astype(BF16)
    from_z(dq_buf, rdq, scale, dq_o)

    for o in z_order:
        zp = z_peer[o]
        arrive(fz_buf.at[zp], rfz.at[zp], z_dev(zp))
    total = fz_buf[0]
    for i in range(1, NZ):
        total = total + fz_buf[i]
    gf_o[...] = total

    for copy in sends:
        copy.wait_send()

    @pl.when(ctx < last)
    def _():
        pltpu.make_async_remote_copy(
            src_ref=win.at[pl.ds(rows, rows)], dst_ref=win.at[pl.ds(0, rows)],
            send_sem=ssem.at[ssem.shape[0] - 1], recv_sem=rhalo,
            device_id=(after, ch), device_id_type=MESH,
        ).wait_send()


def solution(mesh):
    NZ, NY = mesh.shape["ctx"] // NX, mesh.shape["ch"] // NC

    def on_device(go, gi, ci, filt, q, k, cot):
        rows, chans = go.shape
        groups, taps = filt.shape
        heads = chans // HEAD_DIM
        keys, stats = NX * rows, NZ * heads
        n_send = 4 * (NX - 1) + 6 * (NZ - 1) + 2 * NY + (NX - 1) + (NZ - 1) + 1
        vmem, sem = pltpu.VMEM, pltpu.SemaphoreType.DMA
        block = jax.ShapeDtypeStruct((rows, chans), BF16)
        return pl.pallas_call(
            functools.partial(kernel, NZ, NY),
            out_shape=[block] * 4 + [jax.ShapeDtypeStruct((groups, taps), F32)],
            in_specs=[pl.BlockSpec(memory_space=vmem)] * 7,
            out_specs=[pl.BlockSpec(memory_space=vmem)] * 5,
            scratch_shapes=[
                vmem((keys, chans), BF16), vmem((keys, chans), BF16),
                vmem((NZ, rows, chans), BF16), vmem((NZ, rows, chans), BF16),
                vmem((2 * rows, chans), BF16), vmem((groups * rows, 2 * taps), BF16),
                vmem((stats, keys, rows), F32), vmem((stats, keys, rows), F32),
                vmem((heads, keys, NZ * rows), BF16), vmem((heads, keys, NZ * rows), BF16),
                vmem((NZ, stats, rows), F32), vmem((NZ, stats, rows), F32),
                vmem((2, NC, 8, rows), F32), vmem((2, NY, 8, rows), F32),
                vmem((NX, groups, taps), F32), vmem((NZ, groups, taps), F32),
                vmem((keys, chans), BF16), vmem((NX, rows, chans), BF16),
                vmem((keys, chans), BF16), vmem((NX, rows, chans), BF16),
                vmem((NZ, chans, rows), BF16), vmem((NZ, chans, rows), BF16),
                vmem((NZ, chans, rows), BF16), vmem((NZ, chans, rows), BF16),
                vmem((rows, chans), F32), vmem((rows, chans), F32),
                vmem((2 * rows, chans), BF16), vmem((stats, rows), F32), vmem((stats, rows), F32),
                sem((n_send,)), sem((NX,)), sem((NX,)), sem((NZ,)), sem((NZ,)), sem, sem((NZ,)), sem((NZ,)),
                sem((2,)), sem((2, NY)), sem((NX,)), sem((NX,)), sem((NZ,)), sem((NZ,)), sem((NX,)), sem((NZ,)),
            ],
            compiler_params=pltpu.CompilerParams(
                collective_id=0, has_side_effects=True, vmem_limit_bytes=48 * 1024 * 1024
            ),
            name="hyena",
        )(go, gi, ci, filt, q, k, cot)

    block = P("ctx", "ch")
    return jax.shard_map(
        on_device,
        mesh=mesh,
        in_specs=(block, block, block, P("ch", None), block, block, block),
        out_specs=(block, block, block, block, P("ch", None)),
        check_vma=False,
    )
```

```python
import functools
import math

import jax
import jax.numpy as jnp
from jax import lax
from jax.experimental import pallas as pl
from jax.experimental.pallas import tpu as pltpu
from jax.sharding import PartitionSpec as P

MESH = pl.DeviceIdType.MESH
HEAD_DIM = 128
NEGATIVE = -1e30
EPSILON = 1e-05
VMEM_GRANT = 62 * 1024 * 1024
NX = 4
NC = 2
F32 = jnp.float32
BF16 = jnp.bfloat16

NT = (((1,), (1,)), ((), ()))
NN = (((1,), (0,)), ((), ()))
TN = (((0,), (0,)), ((), ()))


def dot(a, b, dims):
    return lax.dot_general(a, b, dims, preferred_element_type=F32)


def kernel(
    NZ, NY,
    go_h, gi_h, ci_h, filt_h, q_h, k_h, cot_h,
    att_h, dq_h, dk_h, ggo_h, gf_h,
    go, gi, ci, filt, win, win_back, toep, conv_buf, mix_buf,
    k0, v0, q0, c0, k1, v1, q1, c1,
    s0, dp0, s1, dp1, p0, ds0, p1, ds1,
    lse0_buf, d0_buf, lse0_sum, d0_sum, part1, lse1_buf, d1_buf,
    core_buf, y_buf, fx_buf, fz_buf,
    dv0_src, dk0_src, dv1_src, dk1_src, att0_src, dq0_src, att1_src, dq1_src,
    dv0_buf, dk0_buf, dv1_buf, dk1_buf, att0_buf, dq0_buf, att1_buf, dq1_buf,
    att_o, dq_o, dk_o, ggo_o, gf_o,
    rload, rstore, ssem, rx, rz, ry, rcore, rhalo, sz,
):
    rows, chans = go_h.shape
    groups, taps = filt_h.shape
    group_size = chans // groups
    width = chans * NY * NC
    scale = 1.0 / math.sqrt(HEAD_DIM)
    row_keys = NX * rows
    ctx, ch = lax.axis_index("ctx"), lax.axis_index("ch")
    z, x = ctx // NX, ctx % NX
    y, core = ch // NC, ch % NC
    last = NZ * NX - 1
    head0, head1 = slice(0, HEAD_DIM), slice(HEAD_DIM, 2 * HEAD_DIM)

    def z_dev(zp):
        return (zp * NX + x, ch)

    def x_dev(xp):
        return (z * NX + xp, ch)

    def y_dev(yp):
        return (ctx, yp * NC + core)

    sibling = (ctx, y * NC + (1 - core))
    near = lambda n: [o for d in range(1, n // 2 + 1) for o in dict.fromkeys((d, n - d))]
    z_peers = [lax.rem(z + o, NZ) for o in near(NZ)]
    x_peers = [lax.rem(x + o, NX) for o in near(NX)]
    y_peers = [lax.rem(y + o, NY) for o in near(NY)]
    before = (lax.rem(ctx + last, last + 1), ch)
    after = (lax.rem(ctx + 1, last + 1), ch)

    def block(i):
        return pl.ds(pl.multiple_of(i * rows, rows), rows)

    stores = []

    def store(src, dst):
        copy = pltpu.make_async_copy(src, dst, rstore.at[len(stores)])
        stores.append(copy)
        copy.start()

    def remote(src, dst, send_sem, recv_sem, dev):
        return pltpu.make_async_remote_copy(
            src_ref=src, dst_ref=dst, send_sem=send_sem, recv_sem=recv_sem, device_id=dev, device_id_type=MESH
        )

    sends = []

    def push(src, dst, recv_sem, dev):
        copy = remote(src, dst, ssem.at[len(sends)], recv_sem, dev)
        sends.append(copy)
        copy.start()

    def arrive(dst, recv_sem, dev):
        remote(dst, dst, ssem.at[0], recv_sem, dev).wait_recv()

    def push_x(t, src, dst):
        for xp in x_peers:
            push(src(xp), dst, rx.at[t, x], x_dev(xp))

    def arrive_x(t, dst):
        for xp in x_peers:
            arrive(dst(xp), rx.at[t, xp], x_dev(xp))

    def push_z(t, src, dst):
        for zp in z_peers:
            push(src, dst, rz.at[t, z], z_dev(zp))

    def arrive_z(t, dst):
        for zp in z_peers:
            arrive(dst(zp), rz.at[t, zp], z_dev(zp))

    def lower(fn, carry=0):
        return lax.fori_loop(1, z + 1, lambda d, c: fn(z - d, c), carry)

    def higher(fn, carry=0):
        return lax.fori_loop(1, NZ - z, lambda d, c: fn(z + d, c), carry)

    one_way = []

    def push_way(way, t, src, dst):
        def copy(zp):
            return remote(src(zp), dst, sz.at[t, zp], rz.at[t, z], z_dev(zp))

        def start(zp, c):
            copy(zp).start()
            return c

        def finish(zp, c):
            copy(zp).wait_send()
            return c

        way(start)
        one_way.append((way, finish))

    def arrive_way(way, t, dst):
        def wait(zp, c):
            arrive(dst(zp), rz.at[t, zp], z_dev(zp))
            return c

        way(wait)

    barrier = pltpu.get_barrier_semaphore()
    greet = [z_dev(p) for p in z_peers] + [x_dev(p) for p in x_peers] + [y_dev(p) for p in y_peers]
    greet += [sibling, before]
    for dev in greet:
        pl.semaphore_signal(barrier, inc=1, device_id=dev, device_id_type=MESH)

    own_x, own_z = block(x), block(z)
    loads = [
        pltpu.make_async_copy(src, dst, rload.at[i])
        for i, (src, dst) in enumerate([
            (gi_h, gi), (ci_h, ci),
            (k_h.at[:, head0], k0.at[own_x]), (q_h.at[:, head1], q1.at[own_x]),
            (k_h.at[:, head1], k1.at[own_z]), (q_h.at[:, head0], q0.at[own_z]),
            (cot_h.at[:, head1], c1.at[own_x]), (cot_h.at[:, head0], c0.at[own_z]),
            (filt_h, filt), (go_h, go),
        ])
    ]
    for load in loads:
        load.start()

    nothing = jnp.zeros((rows, HEAD_DIM), BF16)

    def clear_lower(zp, c):
        for ref in (q0, c0):
            ref[block(zp)] = nothing
        for ref in (dv1_buf, dk1_buf):
            ref[block(zp)] = nothing
        return c

    def clear_higher(zp, c):
        for ref in (k1, v1, att0_buf, dq0_buf):
            ref[block(zp)] = nothing
        return c

    for load in loads[:2]:
        load.wait()
    win[rows:] = (gi[...].astype(F32) * ci[...].astype(F32)).astype(BF16)
    lower(clear_lower)
    higher(clear_higher)
    for load in loads[2:]:
        load.wait()

    pl.semaphore_wait(barrier, len(greet))

    def halo(dev):
        return remote(win.at[pl.ds(rows, rows)], win.at[pl.ds(0, rows)], ssem.at[ssem.shape[0] - 1], rhalo, dev)

    @pl.when(ctx < last)
    def _():
        halo(after).start()

    push_way(higher, 0, lambda zp: k1.at[own_z], k1.at[own_z])
    push_way(lower, 1, lambda zp: q0.at[own_z], q0.at[own_z])
    push_x(0, lambda xp: k0.at[own_x], k0.at[own_x])
    push_x(1, lambda xp: q1.at[own_x], q1.at[own_x])
    push_way(lower, 2, lambda zp: c0.at[own_z], c0.at[own_z])
    push_x(2, lambda xp: c1.at[own_x], c1.at[own_x])

    flip = (
        lax.broadcasted_iota(jnp.int32, (taps, 2 * taps), 0)
        + lax.broadcasted_iota(jnp.int32, (taps, 2 * taps), 1)
        == taps
    ).astype(F32).astype(BF16)
    turned = dot(filt[...], flip, NN)
    for g in range(groups):
        spread = jnp.broadcast_to(turned[g : g + 1], (rows, 2 * taps))
        spread = pltpu.roll(spread, 0, 1, stride=1, stride_axis=0)
        toep[g * rows : (g + 1) * rows] = spread.astype(BF16)
    p0[...] = jnp.zeros_like(p0)
    ds0[...] = jnp.zeros_like(ds0)
    p1[...] = jnp.zeros_like(p1)
    ds1[...] = jnp.zeros_like(ds1)
    lse0_buf[z] = jnp.full((NZ, rows), NEGATIVE, F32)
    d0_buf[z] = jnp.zeros((NZ, rows), F32)
    part1[...] = jnp.full(part1.shape, NEGATIVE, F32)

    @pl.when(ctx > 0)
    def _():
        halo(before).wait_recv()

    @pl.when(ctx == 0)
    def _():
        win[:rows] = jnp.zeros((rows, chans), BF16)

    lane_group = lax.broadcasted_iota(jnp.int32, (rows, chans), 1) // group_size
    window = win[...]
    conv = jnp.zeros((rows, chans), F32)
    for g in range(groups):
        part = dot(toep[g * rows : (g + 1) * rows], window, NN)
        conv = jnp.where(lane_group == g, part, conv)
    conv_buf[...] = conv
    mixer = go[...].astype(F32) * conv
    mix_buf[...] = mixer

    def as_row(column):
        return jnp.broadcast_to(column, (rows, 128)).T[:8]

    def as_tile(row):
        tile = jnp.broadcast_to(row[0:1], (128, rows)).T
        return jnp.concatenate([tile] * (chans // 128), axis=1)

    def to_y(phase, column):
        core_buf[phase, core] = as_row(column)
        push(core_buf.at[phase, core], core_buf.at[phase, core], rcore.at[phase], sibling)
        arrive(core_buf.at[phase, 1 - core], rcore.at[phase], sibling)
        y_buf[phase, y] = core_buf[phase, 0] + core_buf[phase, 1]
        for yp in y_peers:
            push(y_buf.at[phase, y], y_buf.at[phase, y], ry.at[phase, y], y_dev(yp))

    def from_y(phase):
        for yp in y_peers:
            arrive(y_buf.at[phase, yp], ry.at[phase, yp], y_dev(yp))
        total = y_buf[phase, 0]
        for i in range(1, NY):
            total = total + y_buf[phase, i]
        return as_tile(total)

    to_y(0, jnp.sum(mixer * mixer, axis=1, keepdims=True))
    back = (
        lax.broadcasted_iota(jnp.int32, (2 * rows, 2 * rows), 0)
        + lax.broadcasted_iota(jnp.int32, (2 * rows, 2 * rows), 1)
        == 2 * rows - 1
    ).astype(F32).astype(BF16)
    win_back[...] = dot(back, window, NN).astype(BF16)

    def ahead(shape):
        return lax.broadcasted_iota(jnp.int32, shape, 1) - lax.broadcasted_iota(jnp.int32, shape, 0)

    def totals(scores):
        top = jnp.max(scores, axis=0, keepdims=True)
        return top + jnp.log(jnp.sum(jnp.exp(scores - top), axis=0, keepdims=True))

    def score0(zp):
        scores = dot(k0[...], q0[block(zp)], NT) * scale
        scores = jnp.where(ahead(scores.shape) >= (z - zp) * row_keys - x * rows, scores, NEGATIVE)
        s0[zp] = scores
        lse0_buf[z, pl.ds(zp, 1), :] = totals(scores)

    def score1(zp):
        scores = dot(k1[block(zp)], q1[...], NT) * scale
        scores = jnp.where(ahead(scores.shape) >= (zp - z) * row_keys + x * rows, scores, NEGATIVE)
        s1[zp] = scores
        part1[pl.ds(zp, 1), :] = totals(scores)

    def score0_step(zp, c):
        arrive(q0.at[block(zp)], rz.at[1, zp], z_dev(zp))
        score0(zp)
        return c

    def score1_step(zp, c):
        arrive(k1.at[block(zp)], rz.at[0, zp], z_dev(zp))
        score1(zp)
        return c

    arrive_x(0, lambda xp: k0.at[block(xp)])
    score0(z)
    arrive_x(1, lambda xp: q1.at[block(xp)])
    score1(z)

    inv = lax.rsqrt(from_y(0) / width + EPSILON)
    values = (mix_buf[...] * inv).astype(BF16)
    v0[own_x] = values[:, head0]
    v1[own_z] = values[:, head1]
    push_way(higher, 3, lambda zp: v1.at[own_z], v1.at[own_z])
    push_x(3, lambda xp: v0.at[own_x], v0.at[own_x])

    def as_rows(line):
        cut = [line[:, i * rows : (i + 1) * rows] for i in range(NX)]
        return jnp.concatenate(cut + [jnp.zeros((8 - NX, rows), F32)], axis=0)

    def as_line(table):
        return jnp.concatenate([table[i : i + 1] for i in range(NX)], axis=1)

    def log_sum(parts):
        top = jnp.max(parts, axis=0, keepdims=True)
        return (top + jnp.log(jnp.sum(jnp.exp(parts - top), axis=0, keepdims=True)))

    lower(score1_step)
    lse1_buf[x] = as_rows(log_sum(part1[...]))
    push_x(4, lambda xp: lse1_buf.at[x], lse1_buf.at[x])
    higher(score0_step)
    push_z(4, lse0_buf.at[z], lse0_buf.at[z])

    arrive_x(2, lambda xp: c1.at[block(xp)])
    arrive_x(4, lambda xp: lse1_buf.at[xp])
    lse1 = as_line(log_sum(lse1_buf[...])[0])

    def prob1(zp, c):
        weights = jnp.exp(s1[zp] - lse1)
        s1[zp] = weights
        low = weights.astype(BF16)
        p1[block(zp)] = low
        dv1_src[block(zp)] = dot(low, c1[...], NN).astype(BF16)
        return c

    prob1(z, 0)
    lower(prob1)
    push_way(lower, 5, lambda zp: dv1_src.at[block(zp)], dv1_buf.at[own_z])
    dv1_buf[own_z] = dv1_src[own_z]

    arrive_way(higher, 2, lambda zp: c0.at[block(zp)])
    arrive_z(4, lambda zp: lse0_buf.at[zp])
    lse0_sum[...] = log_sum(lse0_buf[...])[0]

    def prob0(zp, c):
        weights = jnp.exp(s0[zp] - lse0_sum[pl.ds(zp, 1), :])
        s0[zp] = weights
        p0[:, block(zp)] = weights.astype(BF16)
        return c

    prob0(z, 0)
    higher(prob0)
    dv0_src[...] = dot(p0[...], c0[...], NN).astype(BF16)
    push_x(5, lambda xp: dv0_src.at[block(xp)], dv0_buf.at[own_x])
    dv0_buf[own_x] = dv0_src[own_x]

    def dprob1(zp, total):
        dprob = dot(v1[block(zp)], c1[...], NT)
        dp1[zp] = dprob
        return total + jnp.sum(s1[zp] * dprob, axis=0, keepdims=True)

    def dprob0(zp, c):
        dprob = dot(v0[...], c0[block(zp)], NT)
        dp0[zp] = dprob
        d0_buf[z, pl.ds(zp, 1), :] = jnp.sum(s0[zp] * dprob, axis=0, keepdims=True)
        return c

    arrive_x(3, lambda xp: v0.at[block(xp)])
    dprob0(z, 0)
    higher(dprob0)
    push_z(6, d0_buf.at[z], d0_buf.at[z])

    arrive_way(lower, 3, lambda zp: v1.at[block(zp)])
    d1_buf[x] = as_rows(lower(dprob1, dprob1(z, jnp.zeros((1, row_keys), F32))))
    push_x(6, lambda xp: d1_buf.at[x], d1_buf.at[x])

    def across(src, keys, low, count):
        full = dot(keys[...], low[...], TN).astype(BF16)
        for i in range(count):
            src[i * HEAD_DIM : (i + 1) * HEAD_DIM] = full[:, i * rows : (i + 1) * rows]

    across(att0_src, v0, p0, NZ)
    push_way(higher, 7, lambda zp: att0_src.at[block(zp)], att0_buf.at[own_z])
    att0_buf[own_z] = att0_src[own_z]
    across(att1_src, v1, p1, NX)
    push_x(7, lambda xp: att1_src.at[block(xp)], att1_buf.at[own_x])
    att1_buf[own_x] = att1_src[own_x]

    def added(ref, count):
        total = ref[:rows].astype(F32)
        for i in range(1, count):
            total = total + ref[i * rows : (i + 1) * rows].astype(F32)
        return total

    arrive_way(higher, 5, lambda zp: dv1_buf.at[block(zp)])
    arrive_x(5, lambda xp: dv0_buf.at[block(xp)])
    value_grad = jnp.concatenate([added(dv0_buf, NX), added(dv1_buf, NZ)], axis=1)
    to_y(1, jnp.sum(value_grad * mix_buf[...], axis=1, keepdims=True))

    arrive_z(6, lambda zp: d0_buf.at[zp])
    delta0 = d0_buf[0]
    for i in range(1, NZ):
        delta0 = delta0 + d0_buf[i]
    d0_sum[...] = delta0

    def dscore0(zp, c):
        dscore = s0[zp] * (dp0[zp] - d0_sum[pl.ds(zp, 1), :])
        ds0[:, block(zp)] = dscore.astype(BF16)
        return c

    dscore0(z, 0)
    higher(dscore0)
    across(dq0_src, k0, ds0, NZ)
    push_way(higher, 8, lambda zp: dq0_src.at[block(zp)], dq0_buf.at[own_z])
    dq0_buf[own_z] = dq0_src[own_z]

    arrive_x(6, lambda xp: d1_buf.at[xp])
    delta1 = d1_buf[0]
    for i in range(1, NX):
        delta1 = delta1 + d1_buf[i]
    delta1 = as_line(delta1)

    def dscore1(zp, c):
        low = (s1[zp] * (dp1[zp] - delta1)).astype(BF16)
        ds1[block(zp)] = low
        dk1_src[block(zp)] = dot(low, q1[...], NN).astype(BF16)
        return c

    dscore1(z, 0)
    lower(dscore1)
    push_way(lower, 9, lambda zp: dk1_src.at[block(zp)], dk1_buf.at[own_z])
    dk1_buf[own_z] = dk1_src[own_z]
    dk0_src[...] = dot(ds0[...], q0[...], NN).astype(BF16)
    push_x(8, lambda xp: dk0_src.at[block(xp)], dk0_buf.at[own_x])
    dk0_buf[own_x] = dk0_src[own_x]
    across(dq1_src, k1, ds1, NX)
    push_x(9, lambda xp: dq1_src.at[block(xp)], dq1_buf.at[own_x])
    dq1_buf[own_x] = dq1_src[own_x]

    proj = from_y(1)
    mixer_grad = inv * value_grad - mix_buf[...] * (inv * inv * inv * proj / width)
    ggo_o[...] = (mixer_grad * conv_buf[...]).astype(BF16)
    store(ggo_o, ggo_h)
    conv_grad = (mixer_grad * go[...].astype(F32)).astype(BF16).astype(F32)
    sums = []
    for g in range(groups):
        pairs = dot(jnp.where(lane_group == g, conv_grad, 0.0).astype(BF16), win_back[...], NT)
        pairs = pltpu.roll(pairs, 1, 1, stride=1, stride_axis=0)
        sums.append(jnp.sum(pairs[:, taps:], axis=0, keepdims=True))
    fx_buf[x] = jnp.concatenate(sums, axis=0)
    push_x(10, lambda xp: fx_buf.at[x], fx_buf.at[x])
    arrive_x(10, lambda xp: fx_buf.at[xp])
    total = fx_buf[0]
    for i in range(1, NX):
        total = total + fx_buf[i]
    fz_buf[z] = total
    push_z(10, fz_buf.at[z], fz_buf.at[z])

    arrive_x(7, lambda xp: att1_buf.at[block(xp)])
    att_o[:, head1] = added(att1_buf, NX).T.astype(BF16)
    arrive_way(lower, 7, lambda zp: att0_buf.at[block(zp)])
    att_o[:, head0] = added(att0_buf, NZ).T.astype(BF16)
    store(att_o, att_h)
    arrive_x(8, lambda xp: dk0_buf.at[block(xp)])
    dk_o[:, head0] = (added(dk0_buf, NX) * scale).astype(BF16)
    arrive_way(higher, 9, lambda zp: dk1_buf.at[block(zp)])
    dk_o[:, head1] = (added(dk1_buf, NZ) * scale).astype(BF16)
    store(dk_o, dk_h)
    arrive_x(9, lambda xp: dq1_buf.at[block(xp)])
    dq_o[:, head1] = (added(dq1_buf, NX).T * scale).astype(BF16)
    arrive_way(lower, 8, lambda zp: dq0_buf.at[block(zp)])
    dq_o[:, head0] = (added(dq0_buf, NZ).T * scale).astype(BF16)
    store(dq_o, dq_h)

    arrive_z(10, lambda zp: fz_buf.at[zp])
    total = fz_buf[0]
    for i in range(1, NZ):
        total = total + fz_buf[i]
    gf_o[...] = total
    store(gf_o, gf_h)

    for copy in sends:
        copy.wait_send()
    for way, finish in one_way:
        way(finish)
    for copy in stores:
        copy.wait()

    @pl.when(ctx < last)
    def _():
        halo(after).wait_send()


def write_out(*refs):
    held, sems = refs[10:15], refs[15]
    loads = [pltpu.make_async_copy(refs[i], held[i], sems.at[i]) for i in range(5)]
    stores = [pltpu.make_async_copy(held[i], refs[5 + i], sems.at[5 + i]) for i in range(5)]
    for load in loads:
        load.start()
    for load, store in zip(loads, stores):
        load.wait()
        store.start()
    for store in stores:
        store.wait()


def solution(mesh):
    NZ, NY = mesh.shape["ctx"] // NX, mesh.shape["ch"] // NC

    def on_device(go, gi, ci, filt, q, k, cot):
        rows, chans = go.shape
        groups, taps = filt.shape
        along_x, along_z = NX * rows, NZ * rows
        n_send = 11 * (NX - 1) + 3 * (NZ - 1) + 2 * NY + 1
        vmem, sem = pltpu.VMEM, pltpu.SemaphoreType.DMA
        block = jax.ShapeDtypeStruct((rows, chans), BF16)
        outs = [block] * 4 + [jax.ShapeDtypeStruct((groups, taps), F32)]
        own = vmem((rows, chans), BF16)
        row_x, row_z = vmem((along_x, HEAD_DIM), BF16), vmem((along_z, HEAD_DIM), BF16)
        results = pl.pallas_call(
            functools.partial(kernel, NZ, NY),
            out_shape=outs,
            in_specs=[pl.BlockSpec(memory_space=pltpu.HBM)] * 7,
            out_specs=[pl.BlockSpec(memory_space=pltpu.HBM)] * 5,
            scratch_shapes=[
                own, own, own, vmem((groups, taps), BF16),
                vmem((2 * rows, chans), BF16), vmem((2 * rows, chans), BF16), vmem((groups * rows, 2 * taps), BF16),
                vmem((rows, chans), F32), vmem((rows, chans), F32),
                row_x, row_x, row_z, row_z, row_z, row_z, row_x, row_x,
                vmem((NZ, along_x, rows), F32), vmem((NZ, along_x, rows), F32),
                vmem((NZ, rows, along_x), F32), vmem((NZ, rows, along_x), F32),
                vmem((along_x, along_z), BF16), vmem((along_x, along_z), BF16),
                vmem((along_z, along_x), BF16), vmem((along_z, along_x), BF16),
                vmem((NZ, NZ, rows), F32), vmem((NZ, NZ, rows), F32), vmem((NZ, rows), F32), vmem((NZ, rows), F32),
                vmem((NZ, along_x), F32), vmem((NX, 8, rows), F32), vmem((NX, 8, rows), F32),
                vmem((2, NC, 8, rows), F32), vmem((2, NY, 8, rows), F32),
                vmem((NX, groups, taps), F32), vmem((NZ, groups, taps), F32),
                row_x, row_x, row_z, row_z, row_z, row_z, row_x, row_x,
                row_x, row_x, row_z, row_z, row_z, row_z, row_x, row_x,
                own, own, own, own, vmem((groups, taps), F32),
                sem((10,)), sem((5,)), sem((n_send,)), sem((11, NX)), sem((11, NZ)), sem((2, NY)), sem((2,)), sem,
                sem((11, NZ)),
            ],
            compiler_params=pltpu.CompilerParams(
                collective_id=0, has_side_effects=True, vmem_limit_bytes=VMEM_GRANT
            ),
            name="hyena",
        )(go, gi, ci, filt, q, k, cot)
        return pl.pallas_call(
            write_out,
            out_shape=outs,
            in_specs=[pl.BlockSpec(memory_space=pltpu.HBM)] * 5,
            out_specs=[pl.BlockSpec(memory_space=pltpu.HBM)] * 5,
            scratch_shapes=[vmem(o.shape, o.dtype) for o in outs] + [sem((10,))],
            compiler_params=pltpu.CompilerParams(vmem_limit_bytes=VMEM_GRANT),
            name="write_out",
        )(*results)

    block = P("ctx", "ch")
    return jax.shard_map(
        on_device,
        mesh=mesh,
        in_specs=(block, block, block, P("ch", None), block, block, block),
        out_specs=(block, block, block, block, P("ch", None)),
        check_vma=False,
    )
```

```python
import functools
import math

import jax
import jax.numpy as jnp
from jax import lax
from jax.experimental import pallas as pl
from jax.experimental.pallas import tpu as pltpu
from jax.sharding import PartitionSpec as P

MESH = pl.DeviceIdType.MESH
HEAD_DIM = 128
NEGATIVE = -1e30
EPSILON = 1e-05
VMEM_GRANT = 62 * 1024 * 1024
NX = 4
NC = 2
F32 = jnp.float32
BF16 = jnp.bfloat16

NT = (((1,), (1,)), ((), ()))
NN = (((1,), (0,)), ((), ()))
TN = (((0,), (0,)), ((), ()))


def dot(a, b, dims):
    return lax.dot_general(a, b, dims, preferred_element_type=F32)


def kernel(
    NZ, NY,
    go_h, gi_h, ci_h, filt_h, q_h, k_h, cot_h,
    att_h, dq_h, dk_h, ggo_h, gf_h,
    go, gi, ci, filt, win, win_back, toep, conv_buf, mix_buf,
    k0, v0, q0, c0, k1, v1, q1, c1,
    s0, dp0, s1, dp1, p0, ds0, p1, ds1,
    lse0_buf, d0_buf, lse0_sum, d0_sum, top0, top1, part1, lse1_buf, d1_buf,
    core_buf, y_buf, fx_buf, fz_buf,
    dv0_src, dk0_src, dv1_src, dk1_src, att0_src, dq0_src, att1_src, dq1_src,
    dv0_buf, dk0_buf, dv1_buf, dk1_buf, att0_buf, dq0_buf, att1_buf, dq1_buf,
    att_o, dq_o, dk_o, ggo_o, gf_o,
    rload, rstore, ssem, rx, rz, ry, rcore, rhalo, sz,
):
    rows, chans = go_h.shape
    groups, taps = filt_h.shape
    group_size = chans // groups
    width = chans * NY * NC
    scale = 1.0 / math.sqrt(HEAD_DIM)
    row_keys = NX * rows
    ctx, ch = lax.axis_index("ctx"), lax.axis_index("ch")
    z, x = ctx // NX, ctx % NX
    y, core = ch // NC, ch % NC
    last = NZ * NX - 1
    head0, head1 = slice(0, HEAD_DIM), slice(HEAD_DIM, 2 * HEAD_DIM)

    def z_dev(zp):
        return (zp * NX + x, ch)

    def x_dev(xp):
        return (z * NX + xp, ch)

    def y_dev(yp):
        return (ctx, yp * NC + core)

    sibling = (ctx, y * NC + (1 - core))
    near = lambda n: [o for d in range(1, n // 2 + 1) for o in dict.fromkeys((d, n - d))]
    z_peers = [lax.rem(z + o, NZ) for o in near(NZ)]
    x_peers = [lax.rem(x + o, NX) for o in near(NX)]
    y_peers = [lax.rem(y + o, NY) for o in near(NY)]
    before = (lax.rem(ctx + last, last + 1), ch)
    after = (lax.rem(ctx + 1, last + 1), ch)

    def block(i):
        return pl.ds(pl.multiple_of(i * rows, rows), rows)

    stores = []

    def store(src, dst):
        copy = pltpu.make_async_copy(src, dst, rstore.at[len(stores)])
        stores.append(copy)
        copy.start()

    def remote(src, dst, send_sem, recv_sem, dev):
        return pltpu.make_async_remote_copy(
            src_ref=src, dst_ref=dst, send_sem=send_sem, recv_sem=recv_sem, device_id=dev, device_id_type=MESH
        )

    sends = []

    def push(src, dst, recv_sem, dev):
        copy = remote(src, dst, ssem.at[len(sends)], recv_sem, dev)
        sends.append(copy)
        copy.start()

    def arrive(dst, recv_sem, dev):
        remote(dst, dst, ssem.at[0], recv_sem, dev).wait_recv()

    def push_x(t, src, dst):
        for xp in x_peers:
            push(src(xp), dst, rx.at[t, x], x_dev(xp))

    def arrive_x(t, dst):
        for xp in x_peers:
            arrive(dst(xp), rx.at[t, xp], x_dev(xp))

    def push_z(t, src, dst):
        for zp in z_peers:
            push(src, dst, rz.at[t, z], z_dev(zp))

    def arrive_z(t, dst):
        for zp in z_peers:
            arrive(dst(zp), rz.at[t, zp], z_dev(zp))

    def lower(fn, carry=0):
        return lax.fori_loop(1, z + 1, lambda d, c: fn(z - d, c), carry)

    def higher(fn, carry=0):
        return lax.fori_loop(1, NZ - z, lambda d, c: fn(z + d, c), carry)

    one_way = []

    def push_way(way, t, src, dst):
        def copy(zp):
            return remote(src(zp), dst, sz.at[t, zp], rz.at[t, z], z_dev(zp))

        def start(zp, c):
            copy(zp).start()
            return c

        def finish(zp, c):
            copy(zp).wait_send()
            return c

        way(start)
        one_way.append((way, finish))

    def arrive_way(way, t, dst):
        def wait(zp, c):
            arrive(dst(zp), rz.at[t, zp], z_dev(zp))
            return c

        way(wait)

    barrier = pltpu.get_barrier_semaphore()
    greet = [z_dev(p) for p in z_peers] + [x_dev(p) for p in x_peers] + [y_dev(p) for p in y_peers]
    greet += [sibling, before]
    for dev in greet:
        pl.semaphore_signal(barrier, inc=1, device_id=dev, device_id_type=MESH)

    own_x, own_z = block(x), block(z)
    loads = [
        pltpu.make_async_copy(src, dst, rload.at[i])
        for i, (src, dst) in enumerate([
            (gi_h, gi), (ci_h, ci),
            (k_h.at[:, head0], k0.at[own_x]), (q_h.at[:, head1], q1.at[own_x]),
            (k_h.at[:, head1], k1.at[own_z]), (q_h.at[:, head0], q0.at[own_z]),
            (cot_h.at[:, head1], c1.at[own_x]), (cot_h.at[:, head0], c0.at[own_z]),
            (filt_h, filt), (go_h, go),
        ])
    ]
    for load in loads:
        load.start()

    nothing = jnp.zeros((rows, HEAD_DIM), BF16)

    def clear_lower(zp, c):
        for ref in (q0, c0):
            ref[block(zp)] = nothing
        for ref in (dv1_buf, dk1_buf):
            ref[block(zp)] = nothing
        return c

    def clear_higher(zp, c):
        for ref in (k1, v1, att0_buf, dq0_buf):
            ref[block(zp)] = nothing
        return c

    for load in loads[:2]:
        load.wait()
    win[rows:] = (gi[...].astype(F32) * ci[...].astype(F32)).astype(BF16)
    lower(clear_lower)
    higher(clear_higher)
    for load in loads[2:]:
        load.wait()

    pl.semaphore_wait(barrier, len(greet))

    def halo(dev):
        return remote(win.at[pl.ds(rows, rows)], win.at[pl.ds(0, rows)], ssem.at[ssem.shape[0] - 1], rhalo, dev)

    @pl.when(ctx < last)
    def _():
        halo(after).start()

    push_way(higher, 0, lambda zp: k1.at[own_z], k1.at[own_z])
    push_way(lower, 1, lambda zp: q0.at[own_z], q0.at[own_z])
    push_x(0, lambda xp: k0.at[own_x], k0.at[own_x])
    push_x(1, lambda xp: q1.at[own_x], q1.at[own_x])
    push_way(lower, 2, lambda zp: c0.at[own_z], c0.at[own_z])
    push_x(2, lambda xp: c1.at[own_x], c1.at[own_x])

    flip = (
        lax.broadcasted_iota(jnp.int32, (taps, 2 * taps), 0)
        + lax.broadcasted_iota(jnp.int32, (taps, 2 * taps), 1)
        == taps
    ).astype(F32).astype(BF16)
    turned = dot(filt[...], flip, NN)
    for g in range(groups):
        spread = jnp.broadcast_to(turned[g : g + 1], (rows, 2 * taps))
        spread = pltpu.roll(spread, 0, 1, stride=1, stride_axis=0)
        toep[g * rows : (g + 1) * rows] = spread.astype(BF16)
    lse0_buf[z] = jnp.full((NZ, rows), NEGATIVE, F32)
    d0_buf[z] = jnp.zeros((NZ, rows), F32)
    part1[...] = jnp.full(part1.shape, NEGATIVE, F32)

    lane_group = lax.broadcasted_iota(jnp.int32, (rows, chans), 1) // group_size

    def conv_part(conv, cols, tokens):
        for g in range(groups):
            part = dot(toep[g * rows : (g + 1) * rows, cols], tokens, NN)
            conv = conv + jnp.where(lane_group == g, part, 0.0)
        return conv

    conv_buf[...] = conv_part(jnp.zeros((rows, chans), F32), slice(rows, 2 * rows), win[rows:])

    @pl.when(ctx > 0)
    def _():
        halo(before).wait_recv()

    @pl.when(ctx == 0)
    def _():
        win[:rows] = jnp.zeros((rows, chans), BF16)

    conv = conv_part(conv_buf[...], slice(0, rows), win[:rows])
    conv_buf[...] = conv
    mixer = go[...].astype(F32) * conv
    mix_buf[...] = mixer

    def as_row(column):
        return jnp.broadcast_to(column, (rows, 128)).T[:8]

    def as_tile(row):
        tile = jnp.broadcast_to(row[0:1], (128, rows)).T
        return jnp.concatenate([tile] * (chans // 128), axis=1)

    def to_y(phase, column):
        core_buf[phase, core] = as_row(column)
        push(core_buf.at[phase, core], core_buf.at[phase, core], rcore.at[phase], sibling)

    def on_to_y(phase):
        arrive(core_buf.at[phase, 1 - core], rcore.at[phase], sibling)
        y_buf[phase, y] = core_buf[phase, 0] + core_buf[phase, 1]
        for yp in y_peers:
            push(y_buf.at[phase, y], y_buf.at[phase, y], ry.at[phase, y], y_dev(yp))

    def from_y(phase):
        for yp in y_peers:
            arrive(y_buf.at[phase, yp], ry.at[phase, yp], y_dev(yp))
        total = y_buf[phase, 0]
        for i in range(1, NY):
            total = total + y_buf[phase, i]
        return as_tile(total)

    to_y(0, jnp.sum(mixer * mixer, axis=1, keepdims=True))
    on_to_y(0)
    back = (
        lax.broadcasted_iota(jnp.int32, (2 * rows, 2 * rows), 0)
        + lax.broadcasted_iota(jnp.int32, (2 * rows, 2 * rows), 1)
        == 2 * rows - 1
    ).astype(F32).astype(BF16)
    win_back[...] = dot(back, win[...], NN).astype(BF16)

    def ahead(shape):
        return lax.broadcasted_iota(jnp.int32, shape, 1) - lax.broadcasted_iota(jnp.int32, shape, 0)

    def totals(scores):
        top = jnp.max(scores, axis=0, keepdims=True)
        powers = jnp.exp(scores - top)
        return top, powers, top + jnp.log(jnp.sum(powers, axis=0, keepdims=True))

    def score0(zp):
        scores = dot(k0[...], q0[block(zp)], NT) * scale
        scores = jnp.where(ahead(scores.shape) >= (z - zp) * row_keys - x * rows, scores, NEGATIVE)
        top0[pl.ds(zp, 1), :], s0[zp], lse0_buf[z, pl.ds(zp, 1), :] = totals(scores)

    def score1(zp):
        scores = dot(k1[block(zp)], q1[...], NT) * scale
        scores = jnp.where(ahead(scores.shape) >= (zp - z) * row_keys + x * rows, scores, NEGATIVE)
        top1[pl.ds(zp, 1), :], s1[zp], part1[pl.ds(zp, 1), :] = totals(scores)

    def score0_step(zp, c):
        arrive(q0.at[block(zp)], rz.at[1, zp], z_dev(zp))
        score0(zp)
        return c

    def score1_step(zp, c):
        arrive(k1.at[block(zp)], rz.at[0, zp], z_dev(zp))
        score1(zp)
        return c

    arrive_x(0, lambda xp: k0.at[block(xp)])
    score0(z)
    arrive_x(1, lambda xp: q1.at[block(xp)])
    score1(z)

    def as_rows(line):
        cut = [line[:, i * rows : (i + 1) * rows] for i in range(NX)]
        return jnp.concatenate(cut + [jnp.zeros((8 - NX, rows), F32)], axis=0)

    def as_line(table):
        return jnp.concatenate([table[i : i + 1] for i in range(NX)], axis=1)

    def log_sum(parts):
        top = jnp.max(parts, axis=0, keepdims=True)
        return (top + jnp.log(jnp.sum(jnp.exp(parts - top), axis=0, keepdims=True)))

    lower(score1_step)
    lse1_buf[x] = as_rows(log_sum(part1[...]))
    push_x(4, lambda xp: lse1_buf.at[x], lse1_buf.at[x])
    higher(score0_step)
    push_z(4, lse0_buf.at[z], lse0_buf.at[z])

    inv = lax.rsqrt(from_y(0) / width + EPSILON)
    values = (mix_buf[...] * inv).astype(BF16)
    v0[own_x] = values[:, head0]
    v1[own_z] = values[:, head1]
    push_way(higher, 3, lambda zp: v1.at[own_z], v1.at[own_z])
    push_x(3, lambda xp: v0.at[own_x], v0.at[own_x])

    def clear_columns(zp, c):
        p0[:, block(zp)] = jnp.zeros((row_keys, rows), BF16)
        ds0[:, block(zp)] = jnp.zeros((row_keys, rows), BF16)
        return c

    def clear_rows(zp, c):
        p1[block(zp)] = jnp.zeros((rows, row_keys), BF16)
        ds1[block(zp)] = jnp.zeros((rows, row_keys), BF16)
        return c

    lower(clear_columns)
    higher(clear_rows)

    arrive_x(2, lambda xp: c1.at[block(xp)])
    arrive_x(4, lambda xp: lse1_buf.at[xp])
    lse1 = as_line(log_sum(lse1_buf[...])[0])

    def prob1(zp, c):
        weights = s1[zp] * jnp.exp(top1[pl.ds(zp, 1), :] - lse1)
        s1[zp] = weights
        low = weights.astype(BF16)
        p1[block(zp)] = low
        dv1_src[block(zp)] = dot(low, c1[...], NN).astype(BF16)
        return c

    prob1(z, 0)
    lower(prob1)
    push_way(lower, 5, lambda zp: dv1_src.at[block(zp)], dv1_buf.at[own_z])
    dv1_buf[own_z] = dv1_src[own_z]

    arrive_way(higher, 2, lambda zp: c0.at[block(zp)])
    arrive_z(4, lambda zp: lse0_buf.at[zp])
    lse0_sum[...] = log_sum(lse0_buf[...])[0]

    def prob0(zp, c):
        weights = s0[zp] * jnp.exp(top0[pl.ds(zp, 1), :] - lse0_sum[pl.ds(zp, 1), :])
        s0[zp] = weights
        p0[:, block(zp)] = weights.astype(BF16)
        return c

    prob0(z, 0)
    higher(prob0)
    dv0_src[...] = dot(p0[...], c0[...], NN).astype(BF16)
    push_x(5, lambda xp: dv0_src.at[block(xp)], dv0_buf.at[own_x])
    dv0_buf[own_x] = dv0_src[own_x]

    def dprob1(zp, total):
        dprob = dot(v1[block(zp)], c1[...], NT)
        dp1[zp] = dprob
        return total + jnp.sum(s1[zp] * dprob, axis=0, keepdims=True)

    def dprob0(zp, c):
        dprob = dot(v0[...], c0[block(zp)], NT)
        dp0[zp] = dprob
        d0_buf[z, pl.ds(zp, 1), :] = jnp.sum(s0[zp] * dprob, axis=0, keepdims=True)
        return c

    arrive_x(3, lambda xp: v0.at[block(xp)])
    dprob0(z, 0)
    higher(dprob0)
    push_z(6, d0_buf.at[z], d0_buf.at[z])

    arrive_way(lower, 3, lambda zp: v1.at[block(zp)])
    d1_buf[x] = as_rows(lower(dprob1, dprob1(z, jnp.zeros((1, row_keys), F32))))
    push_x(6, lambda xp: d1_buf.at[x], d1_buf.at[x])

    def across(src, keys, low, count):
        full = dot(keys[...], low[...], TN).astype(BF16)
        for i in range(count):
            src[i * HEAD_DIM : (i + 1) * HEAD_DIM] = full[:, i * rows : (i + 1) * rows]

    across(att0_src, v0, p0, NZ)
    push_way(higher, 7, lambda zp: att0_src.at[block(zp)], att0_buf.at[own_z])
    att0_buf[own_z] = att0_src[own_z]

    def added(ref, count):
        total = ref[:rows].astype(F32)
        for i in range(1, count):
            total = total + ref[i * rows : (i + 1) * rows].astype(F32)
        return total

    arrive_way(higher, 5, lambda zp: dv1_buf.at[block(zp)])
    arrive_x(5, lambda xp: dv0_buf.at[block(xp)])
    value_grad = jnp.concatenate([added(dv0_buf, NX), added(dv1_buf, NZ)], axis=1)
    to_y(1, jnp.sum(value_grad * mix_buf[...], axis=1, keepdims=True))
    across(att1_src, v1, p1, NX)
    push_x(7, lambda xp: att1_src.at[block(xp)], att1_buf.at[own_x])
    att1_buf[own_x] = att1_src[own_x]
    on_to_y(1)

    arrive_z(6, lambda zp: d0_buf.at[zp])
    delta0 = d0_buf[0]
    for i in range(1, NZ):
        delta0 = delta0 + d0_buf[i]
    d0_sum[...] = delta0

    def dscore0(zp, c):
        dscore = s0[zp] * (dp0[zp] - d0_sum[pl.ds(zp, 1), :])
        ds0[:, block(zp)] = dscore.astype(BF16)
        return c

    dscore0(z, 0)
    higher(dscore0)
    across(dq0_src, k0, ds0, NZ)
    push_way(higher, 8, lambda zp: dq0_src.at[block(zp)], dq0_buf.at[own_z])
    dq0_buf[own_z] = dq0_src[own_z]

    arrive_x(6, lambda xp: d1_buf.at[xp])
    delta1 = d1_buf[0]
    for i in range(1, NX):
        delta1 = delta1 + d1_buf[i]
    delta1 = as_line(delta1)

    def dscore1(zp, c):
        low = (s1[zp] * (dp1[zp] - delta1)).astype(BF16)
        ds1[block(zp)] = low
        dk1_src[block(zp)] = dot(low, q1[...], NN).astype(BF16)
        return c

    dscore1(z, 0)
    lower(dscore1)
    push_way(lower, 9, lambda zp: dk1_src.at[block(zp)], dk1_buf.at[own_z])
    dk1_buf[own_z] = dk1_src[own_z]
    dk0_src[...] = dot(ds0[...], q0[...], NN).astype(BF16)
    push_x(8, lambda xp: dk0_src.at[block(xp)], dk0_buf.at[own_x])
    dk0_buf[own_x] = dk0_src[own_x]
    across(dq1_src, k1, ds1, NX)
    push_x(9, lambda xp: dq1_src.at[block(xp)], dq1_buf.at[own_x])
    dq1_buf[own_x] = dq1_src[own_x]

    proj = from_y(1)
    mixer_grad = inv * value_grad - mix_buf[...] * (inv * inv * inv * proj / width)
    conv_grad = (mixer_grad * go[...].astype(F32)).astype(BF16).astype(F32)
    sums = []
    for g in range(groups):
        pairs = dot(jnp.where(lane_group == g, conv_grad, 0.0).astype(BF16), win_back[...], NT)
        pairs = pltpu.roll(pairs, 1, 1, stride=1, stride_axis=0)
        sums.append(jnp.sum(pairs[:, taps:], axis=0, keepdims=True))
    fx_buf[x] = jnp.concatenate(sums, axis=0).astype(BF16)
    push_x(10, lambda xp: fx_buf.at[x], fx_buf.at[x])
    ggo_o[...] = (mixer_grad * conv_buf[...]).astype(BF16)
    store(ggo_o, ggo_h)
    arrive_x(7, lambda xp: att1_buf.at[block(xp)])
    att_o[:, head1] = added(att1_buf, NX).T.astype(BF16)
    arrive_way(lower, 7, lambda zp: att0_buf.at[block(zp)])
    att_o[:, head0] = added(att0_buf, NZ).T.astype(BF16)
    store(att_o, att_h)
    arrive_x(10, lambda xp: fx_buf.at[xp])
    total = fx_buf[0].astype(F32)
    for i in range(1, NX):
        total = total + fx_buf[i].astype(F32)
    fz_buf[z] = total.astype(BF16)
    push_z(10, fz_buf.at[z], fz_buf.at[z])

    arrive_x(8, lambda xp: dk0_buf.at[block(xp)])
    dk_o[:, head0] = (added(dk0_buf, NX) * scale).astype(BF16)
    arrive_way(higher, 9, lambda zp: dk1_buf.at[block(zp)])
    dk_o[:, head1] = (added(dk1_buf, NZ) * scale).astype(BF16)
    store(dk_o, dk_h)
    arrive_x(9, lambda xp: dq1_buf.at[block(xp)])
    dq_o[:, head1] = (added(dq1_buf, NX).T * scale).astype(BF16)
    arrive_way(lower, 8, lambda zp: dq0_buf.at[block(zp)])
    dq_o[:, head0] = (added(dq0_buf, NZ).T * scale).astype(BF16)
    store(dq_o, dq_h)

    arrive_z(10, lambda zp: fz_buf.at[zp])
    total = fz_buf[0].astype(F32)
    for i in range(1, NZ):
        total = total + fz_buf[i].astype(F32)
    gf_o[...] = total
    store(gf_o, gf_h)

    for copy in sends:
        copy.wait_send()
    for way, finish in one_way:
        way(finish)
    for copy in stores:
        copy.wait()

    @pl.when(ctx < last)
    def _():
        halo(after).wait_send()


def write_out(*refs):
    held, sems = refs[10:15], refs[15]
    loads = [pltpu.make_async_copy(refs[i], held[i], sems.at[i]) for i in range(5)]
    stores = [pltpu.make_async_copy(held[i], refs[5 + i], sems.at[5 + i]) for i in range(5)]
    for load in loads:
        load.start()
    for load, store in zip(loads, stores):
        load.wait()
        store.start()
    for store in stores:
        store.wait()


def solution(mesh):
    NZ, NY = mesh.shape["ctx"] // NX, mesh.shape["ch"] // NC

    def on_device(go, gi, ci, filt, q, k, cot):
        rows, chans = go.shape
        groups, taps = filt.shape
        along_x, along_z = NX * rows, NZ * rows
        n_send = 11 * (NX - 1) + 3 * (NZ - 1) + 2 * NY + 1
        vmem, sem = pltpu.VMEM, pltpu.SemaphoreType.DMA
        block = jax.ShapeDtypeStruct((rows, chans), BF16)
        outs = [block] * 4 + [jax.ShapeDtypeStruct((groups, taps), F32)]
        own = vmem((rows, chans), BF16)
        row_x, row_z = vmem((along_x, HEAD_DIM), BF16), vmem((along_z, HEAD_DIM), BF16)
        results = pl.pallas_call(
            functools.partial(kernel, NZ, NY),
            out_shape=outs,
            in_specs=[pl.BlockSpec(memory_space=pltpu.HBM)] * 7,
            out_specs=[pl.BlockSpec(memory_space=pltpu.HBM)] * 5,
            scratch_shapes=[
                own, own, own, vmem((groups, taps), BF16),
                vmem((2 * rows, chans), BF16), vmem((2 * rows, chans), BF16), vmem((groups * rows, 2 * taps), BF16),
                vmem((rows, chans), F32), vmem((rows, chans), F32),
                row_x, row_x, row_z, row_z, row_z, row_z, row_x, row_x,
                vmem((NZ, along_x, rows), F32), vmem((NZ, along_x, rows), F32),
                vmem((NZ, rows, along_x), F32), vmem((NZ, rows, along_x), F32),
                vmem((along_x, along_z), BF16), vmem((along_x, along_z), BF16),
                vmem((along_z, along_x), BF16), vmem((along_z, along_x), BF16),
                vmem((NZ, NZ, rows), F32), vmem((NZ, NZ, rows), F32), vmem((NZ, rows), F32), vmem((NZ, rows), F32),
                vmem((NZ, rows), F32), vmem((NZ, along_x), F32), vmem((NZ, along_x), F32), vmem((NX, 8, rows), F32), vmem((NX, 8, rows), F32),
                vmem((2, NC, 8, rows), F32), vmem((2, NY, 8, rows), F32),
                vmem((NX, groups, taps), BF16), vmem((NZ, groups, taps), BF16),
                row_x, row_x, row_z, row_z, row_z, row_z, row_x, row_x,
                row_x, row_x, row_z, row_z, row_z, row_z, row_x, row_x,
                own, own, own, own, vmem((groups, taps), F32),
                sem((10,)), sem((5,)), sem((n_send,)), sem((11, NX)), sem((11, NZ)), sem((2, NY)), sem((2,)), sem,
                sem((11, NZ)),
            ],
            compiler_params=pltpu.CompilerParams(
                collective_id=0, has_side_effects=True, vmem_limit_bytes=VMEM_GRANT
            ),
            name="hyena",
        )(go, gi, ci, filt, q, k, cot)
        return pl.pallas_call(
            write_out,
            out_shape=outs,
            in_specs=[pl.BlockSpec(memory_space=pltpu.HBM)] * 5,
            out_specs=[pl.BlockSpec(memory_space=pltpu.HBM)] * 5,
            scratch_shapes=[vmem(o.shape, o.dtype) for o in outs] + [sem((10,))],
            compiler_params=pltpu.CompilerParams(vmem_limit_bytes=VMEM_GRANT),
            name="write_out",
        )(*results)

    block = P("ctx", "ch")
    return jax.shard_map(
        on_device,
        mesh=mesh,
        in_specs=(block, block, block, P("ch", None), block, block, block),
        out_specs=(block, block, block, block, P("ch", None)),
        check_vma=False,
    )
```

```python
import functools
import math

import jax
import jax.numpy as jnp
from jax import lax
from jax.experimental import pallas as pl
from jax.experimental.pallas import tpu as pltpu
from jax.sharding import PartitionSpec as P

MESH = pl.DeviceIdType.MESH
HEAD_DIM = 128
NEGATIVE = -1e30
EPSILON = 1e-05
VMEM_GRANT = 62 * 1024 * 1024
NX = 4
NC = 2
F32 = jnp.float32
BF16 = jnp.bfloat16

NT = (((1,), (1,)), ((), ()))
NN = (((1,), (0,)), ((), ()))
TN = (((0,), (0,)), ((), ()))


def dot(a, b, dims):
    return lax.dot_general(a, b, dims, preferred_element_type=F32)


def kernel(
    NZ, NY,
    go_h, gi_h, ci_h, filt_h, q_h, k_h, cot_h,
    att_h, dq_h, dk_h, ggo_h, gf_h,
    go, gi, ci, filt, win, win_back, toep, conv_buf, mix_buf,
    k0, v0, q0, c0, k1, v1, q1, c1,
    s0, dp0, s1, dp1, p0, ds0, p1, ds1,
    lse0_buf, d0_buf, lse0_sum, d0_sum, top0, top1, part1, lse1_buf, d1_buf,
    core_buf, y_buf, fx_buf, fz_buf,
    dv0_src, dk0_src, dv1_src, dk1_src, att0_src, dq0_src, att1_src, dq1_src,
    dv0_buf, dk0_buf, dv1_buf, dk1_buf, att0_buf, dq0_buf, att1_buf, dq1_buf,
    att_o, dq_o, dk_o, ggo_o, gf_o,
    rload, rstore, sx, rx, sz, rz, sz_all, rz_all, sy, ry, score, rcore, shalo, rhalo,
):
    rows, chans = go_h.shape
    groups, taps = filt_h.shape
    group_size = chans // groups
    width = chans * NY * NC
    scale = 1.0 / math.sqrt(HEAD_DIM)
    row_keys = NX * rows
    ctx, ch = lax.axis_index("ctx"), lax.axis_index("ch")
    z, x = ctx // NX, ctx % NX
    y, core = ch // NC, ch % NC
    last = NZ * NX - 1
    head0, head1 = slice(0, HEAD_DIM), slice(HEAD_DIM, 2 * HEAD_DIM)

    def z_dev(zp):
        return (zp * NX + x, ch)

    def x_dev(xp):
        return (z * NX + xp, ch)

    def y_dev(yp):
        return (ctx, yp * NC + core)

    sibling = (ctx, y * NC + (1 - core))
    near = lambda n: [o for d in range(1, n // 2 + 1) for o in dict.fromkeys((d, n - d))]
    z_peers = [lax.rem(z + o, NZ) for o in near(NZ)]
    x_peers = [lax.rem(x + o, NX) for o in near(NX)]
    y_peers = [lax.rem(y + o, NY) for o in near(NY)]
    before = (lax.rem(ctx + last, last + 1), ch)
    after = (lax.rem(ctx + 1, last + 1), ch)

    def block(i):
        return pl.ds(pl.multiple_of(i * rows, rows), rows)

    stores = []

    def store(src, dst):
        copy = pltpu.make_async_copy(src, dst, rstore.at[len(stores)])
        stores.append(copy)
        copy.start()

    def remote(src, dst, send_sem, recv_sem, dev):
        return pltpu.make_async_remote_copy(
            src_ref=src, dst_ref=dst, send_sem=send_sem, recv_sem=recv_sem, device_id=dev, device_id_type=MESH
        )

    ends = []

    def push(peers, dev, src, dst, send_sem, recv_sem, all_sent):
        for p in peers:
            remote(src(p), dst, send_sem, recv_sem, dev(p)).start()
        ends.append(lambda: remote(all_sent, all_sent, send_sem, recv_sem, dev(peers[0])).wait_send())

    def arrive(dst, recv_sem, dev):
        remote(dst, dst, sx.at[0], recv_sem, dev).wait_recv()

    def push_x(t, src, dst, some):
        push(x_peers, x_dev, src, dst, sx.at[t], rx.at[t], some)

    def arrive_x(t, some):
        arrive(some, rx.at[t], x_dev(x_peers[0]))

    def push_z(t, src, dst, some):
        push(z_peers, z_dev, src, dst, sz_all.at[t], rz_all.at[t], some)

    def arrive_z(t, some):
        arrive(some, rz_all.at[t], z_dev(z_peers[0]))

    def lower(fn, carry=0):
        return lax.fori_loop(1, z + 1, lambda d, c: fn(z - d, c), carry)

    def higher(fn, carry=0):
        return lax.fori_loop(1, NZ - z, lambda d, c: fn(z + d, c), carry)

    one_way = []

    def push_way(way, t, src, dst):
        def copy(zp):
            return remote(src(zp), dst, sz.at[t, zp], rz.at[t, z], z_dev(zp))

        def start(zp, c):
            copy(zp).start()
            return c

        def finish(zp, c):
            copy(zp).wait_send()
            return c

        way(start)
        one_way.append((way, finish))

    def arrive_way(way, t, dst):
        def wait(zp, c):
            arrive(dst(zp), rz.at[t, zp], z_dev(zp))
            return c

        way(wait)

    barrier = pltpu.get_barrier_semaphore()
    greet = [z_dev(p) for p in z_peers] + [x_dev(p) for p in x_peers] + [y_dev(p) for p in y_peers]
    greet += [sibling, before]
    for dev in greet:
        pl.semaphore_signal(barrier, inc=1, device_id=dev, device_id_type=MESH)

    own_x, own_z = block(x), block(z)
    most_x = pl.ds(0, (NX - 1) * rows)
    loads = [
        pltpu.make_async_copy(src, dst, rload.at[i])
        for i, (src, dst) in enumerate([
            (gi_h, gi), (ci_h, ci),
            (k_h.at[:, head0], k0.at[own_x]), (q_h.at[:, head1], q1.at[own_x]),
            (k_h.at[:, head1], k1.at[own_z]), (q_h.at[:, head0], q0.at[own_z]),
            (cot_h.at[:, head1], c1.at[own_x]), (cot_h.at[:, head0], c0.at[own_z]),
            (filt_h, filt), (go_h, go),
        ])
    ]
    for load in loads:
        load.start()

    nothing = jnp.zeros((rows, HEAD_DIM), BF16)

    def clear_lower(zp, c):
        for ref in (q0, c0):
            ref[block(zp)] = nothing
        for ref in (dv1_buf, dk1_buf):
            ref[block(zp)] = nothing
        return c

    def clear_higher(zp, c):
        for ref in (k1, v1, att0_buf, dq0_buf):
            ref[block(zp)] = nothing
        return c

    for load in loads[:2]:
        load.wait()
    win[rows:] = (gi[...].astype(F32) * ci[...].astype(F32)).astype(BF16)
    lower(clear_lower)
    higher(clear_higher)
    for load in loads[2:]:
        load.wait()

    pl.semaphore_wait(barrier, len(greet))

    def halo(dev):
        return remote(win.at[pl.ds(rows, rows)], win.at[pl.ds(0, rows)], shalo, rhalo, dev)

    @pl.when(ctx < last)
    def _():
        halo(after).start()

    push_way(higher, 0, lambda zp: k1.at[own_z], k1.at[own_z])
    push_way(lower, 1, lambda zp: q0.at[own_z], q0.at[own_z])
    push_x(0, lambda xp: k0.at[own_x], k0.at[own_x], k0.at[most_x])
    push_x(1, lambda xp: q1.at[own_x], q1.at[own_x], q1.at[most_x])
    push_way(lower, 2, lambda zp: c0.at[own_z], c0.at[own_z])
    push_x(2, lambda xp: c1.at[own_x], c1.at[own_x], c1.at[most_x])

    flip = (
        lax.broadcasted_iota(jnp.int32, (taps, 2 * taps), 0)
        + lax.broadcasted_iota(jnp.int32, (taps, 2 * taps), 1)
        == taps
    ).astype(F32).astype(BF16)
    turned = dot(filt[...], flip, NN)
    for g in range(groups):
        spread = jnp.broadcast_to(turned[g : g + 1], (rows, 2 * taps))
        spread = pltpu.roll(spread, 0, 1, stride=1, stride_axis=0)
        toep[g * rows : (g + 1) * rows] = spread.astype(BF16)
    lse0_buf[z] = jnp.full((NZ, rows), NEGATIVE, F32)
    d0_buf[z] = jnp.zeros((NZ, rows), F32)
    part1[...] = jnp.full(part1.shape, NEGATIVE, F32)

    lane_group = lax.broadcasted_iota(jnp.int32, (rows, chans), 1) // group_size

    def conv_part(conv, cols, tokens):
        for g in range(groups):
            part = dot(toep[g * rows : (g + 1) * rows, cols], tokens, NN)
            conv = conv + jnp.where(lane_group == g, part, 0.0)
        return conv

    conv_buf[...] = conv_part(jnp.zeros((rows, chans), F32), slice(rows, 2 * rows), win[rows:])

    @pl.when(ctx > 0)
    def _():
        halo(before).wait_recv()

    @pl.when(ctx == 0)
    def _():
        win[:rows] = jnp.zeros((rows, chans), BF16)

    conv = conv_part(conv_buf[...], slice(0, rows), win[:rows])
    conv_buf[...] = conv
    mixer = go[...].astype(F32) * conv
    mix_buf[...] = mixer

    def as_row(column):
        return jnp.broadcast_to(column, (rows, 128)).T[:8]

    def as_tile(row):
        tile = jnp.broadcast_to(row[0:1], (128, rows)).T
        return jnp.concatenate([tile] * (chans // 128), axis=1)

    def to_y(phase, column):
        core_buf[phase, core] = as_row(column)
        own = core_buf.at[phase, core]
        push([0], lambda p: sibling, lambda p: own, own, score.at[phase], rcore.at[phase], own)

    def on_to_y(phase):
        arrive(core_buf.at[phase, 1 - core], rcore.at[phase], sibling)
        y_buf[phase, y] = core_buf[phase, 0] + core_buf[phase, 1]
        own = y_buf.at[phase, y]
        push(y_peers, y_dev, lambda p: own, own, sy.at[phase], ry.at[phase], y_buf.at[phase, pl.ds(0, NY - 1)])

    def from_y(phase):
        arrive(y_buf.at[phase, pl.ds(0, NY - 1)], ry.at[phase], y_dev(y_peers[0]))
        total = y_buf[phase, 0]
        for i in range(1, NY):
            total = total + y_buf[phase, i]
        return as_tile(total)

    to_y(0, jnp.sum(mixer * mixer, axis=1, keepdims=True))
    on_to_y(0)
    back = (
        lax.broadcasted_iota(jnp.int32, (2 * rows, 2 * rows), 0)
        + lax.broadcasted_iota(jnp.int32, (2 * rows, 2 * rows), 1)
        == 2 * rows - 1
    ).astype(F32).astype(BF16)
    win_back[...] = dot(back, win[...], NN).astype(BF16)

    def ahead(shape):
        return lax.broadcasted_iota(jnp.int32, shape, 1) - lax.broadcasted_iota(jnp.int32, shape, 0)

    def totals(scores):
        top = jnp.max(scores, axis=0, keepdims=True)
        powers = jnp.exp(scores - top)
        return top, powers, top + jnp.log(jnp.sum(powers, axis=0, keepdims=True))

    def score0(zp):
        scores = dot(k0[...], q0[block(zp)], NT) * scale
        scores = jnp.where(ahead(scores.shape) >= (z - zp) * row_keys - x * rows, scores, NEGATIVE)
        top0[pl.ds(zp, 1), :], s0[zp], lse0_buf[z, pl.ds(zp, 1), :] = totals(scores)

    def score1(zp):
        scores = dot(k1[block(zp)], q1[...], NT) * scale
        scores = jnp.where(ahead(scores.shape) >= (zp - z) * row_keys + x * rows, scores, NEGATIVE)
        top1[pl.ds(zp, 1), :], s1[zp], part1[pl.ds(zp, 1), :] = totals(scores)

    def score0_step(zp, c):
        arrive(q0.at[block(zp)], rz.at[1, zp], z_dev(zp))
        score0(zp)
        return c

    def score1_step(zp, c):
        arrive(k1.at[block(zp)], rz.at[0, zp], z_dev(zp))
        score1(zp)
        return c

    arrive_x(0, k0.at[most_x])
    score0(z)
    arrive_x(1, q1.at[most_x])
    score1(z)

    def as_rows(line):
        cut = [line[:, i * rows : (i + 1) * rows] for i in range(NX)]
        return jnp.concatenate(cut + [jnp.zeros((8 - NX, rows), F32)], axis=0)

    def as_line(table):
        return jnp.concatenate([table[i : i + 1] for i in range(NX)], axis=1)

    def log_sum(parts):
        top = jnp.max(parts, axis=0, keepdims=True)
        return (top + jnp.log(jnp.sum(jnp.exp(parts - top), axis=0, keepdims=True)))

    lower(score1_step)
    lse1_buf[x] = as_rows(log_sum(part1[...]))
    push_x(4, lambda xp: lse1_buf.at[x], lse1_buf.at[x], lse1_buf.at[pl.ds(0, NX - 1)])
    higher(score0_step)
    push_z(0, lambda zp: lse0_buf.at[z], lse0_buf.at[z], lse0_buf.at[pl.ds(0, NZ - 1)])

    inv = lax.rsqrt(from_y(0) / width + EPSILON)
    values = (mix_buf[...] * inv).astype(BF16)
    v0[own_x] = values[:, head0]
    v1[own_z] = values[:, head1]
    push_way(higher, 3, lambda zp: v1.at[own_z], v1.at[own_z])
    push_x(3, lambda xp: v0.at[own_x], v0.at[own_x], v0.at[most_x])

    def clear_columns(zp, c):
        p0[:, block(zp)] = jnp.zeros((row_keys, rows), BF16)
        ds0[:, block(zp)] = jnp.zeros((row_keys, rows), BF16)
        return c

    def clear_rows(zp, c):
        p1[block(zp)] = jnp.zeros((rows, row_keys), BF16)
        ds1[block(zp)] = jnp.zeros((rows, row_keys), BF16)
        return c

    lower(clear_columns)
    higher(clear_rows)

    arrive_x(2, c1.at[most_x])
    arrive_x(4, lse1_buf.at[pl.ds(0, NX - 1)])
    lse1 = as_line(log_sum(lse1_buf[...])[0])

    def prob1(zp, c):
        weights = s1[zp] * jnp.exp(top1[pl.ds(zp, 1), :] - lse1)
        s1[zp] = weights
        low = weights.astype(BF16)
        p1[block(zp)] = low
        dv1_src[block(zp)] = dot(low, c1[...], NN).astype(BF16)
        return c

    prob1(z, 0)
    lower(prob1)
    push_way(lower, 5, lambda zp: dv1_src.at[block(zp)], dv1_buf.at[own_z])
    dv1_buf[own_z] = dv1_src[own_z]

    arrive_way(higher, 2, lambda zp: c0.at[block(zp)])
    arrive_z(0, lse0_buf.at[pl.ds(0, NZ - 1)])
    lse0_sum[...] = log_sum(lse0_buf[...])[0]

    def prob0(zp, c):
        weights = s0[zp] * jnp.exp(top0[pl.ds(zp, 1), :] - lse0_sum[pl.ds(zp, 1), :])
        s0[zp] = weights
        p0[:, block(zp)] = weights.astype(BF16)
        return c

    prob0(z, 0)
    higher(prob0)
    dv0_src[...] = dot(p0[...], c0[...], NN).astype(BF16)
    push_x(5, lambda xp: dv0_src.at[block(xp)], dv0_buf.at[own_x], dv0_buf.at[most_x])
    dv0_buf[own_x] = dv0_src[own_x]

    def dprob1(zp, total):
        dprob = dot(v1[block(zp)], c1[...], NT)
        dp1[zp] = dprob
        return total + jnp.sum(s1[zp] * dprob, axis=0, keepdims=True)

    def dprob0(zp, c):
        dprob = dot(v0[...], c0[block(zp)], NT)
        dp0[zp] = dprob
        d0_buf[z, pl.ds(zp, 1), :] = jnp.sum(s0[zp] * dprob, axis=0, keepdims=True)
        return c

    arrive_x(3, v0.at[most_x])
    dprob0(z, 0)
    higher(dprob0)
    push_z(1, lambda zp: d0_buf.at[z], d0_buf.at[z], d0_buf.at[pl.ds(0, NZ - 1)])

    arrive_way(lower, 3, lambda zp: v1.at[block(zp)])
    d1_buf[x] = as_rows(lower(dprob1, dprob1(z, jnp.zeros((1, row_keys), F32))))
    push_x(6, lambda xp: d1_buf.at[x], d1_buf.at[x], d1_buf.at[pl.ds(0, NX - 1)])

    def across(src, keys, low, count):
        full = dot(keys[...], low[...], TN).astype(BF16)
        for i in range(count):
            src[i * HEAD_DIM : (i + 1) * HEAD_DIM] = full[:, i * rows : (i + 1) * rows]

    across(att0_src, v0, p0, NZ)
    push_way(higher, 7, lambda zp: att0_src.at[block(zp)], att0_buf.at[own_z])
    att0_buf[own_z] = att0_src[own_z]

    def added(ref, count):
        total = ref[:rows].astype(F32)
        for i in range(1, count):
            total = total + ref[i * rows : (i + 1) * rows].astype(F32)
        return total

    arrive_way(higher, 5, lambda zp: dv1_buf.at[block(zp)])
    arrive_x(5, dv0_buf.at[most_x])
    value_grad = jnp.concatenate([added(dv0_buf, NX), added(dv1_buf, NZ)], axis=1)
    to_y(1, jnp.sum(value_grad * mix_buf[...], axis=1, keepdims=True))
    across(att1_src, v1, p1, NX)
    push_x(7, lambda xp: att1_src.at[block(xp)], att1_buf.at[own_x], att1_buf.at[most_x])
    att1_buf[own_x] = att1_src[own_x]
    on_to_y(1)

    arrive_z(1, d0_buf.at[pl.ds(0, NZ - 1)])
    delta0 = d0_buf[0]
    for i in range(1, NZ):
        delta0 = delta0 + d0_buf[i]
    d0_sum[...] = delta0

    def dscore0(zp, c):
        dscore = s0[zp] * (dp0[zp] - d0_sum[pl.ds(zp, 1), :])
        ds0[:, block(zp)] = dscore.astype(BF16)
        return c

    dscore0(z, 0)
    higher(dscore0)
    across(dq0_src, k0, ds0, NZ)
    push_way(higher, 8, lambda zp: dq0_src.at[block(zp)], dq0_buf.at[own_z])
    dq0_buf[own_z] = dq0_src[own_z]

    arrive_x(6, d1_buf.at[pl.ds(0, NX - 1)])
    delta1 = d1_buf[0]
    for i in range(1, NX):
        delta1 = delta1 + d1_buf[i]
    delta1 = as_line(delta1)

    def dscore1(zp, c):
        low = (s1[zp] * (dp1[zp] - delta1)).astype(BF16)
        ds1[block(zp)] = low
        dk1_src[block(zp)] = dot(low, q1[...], NN).astype(BF16)
        return c

    dscore1(z, 0)
    lower(dscore1)
    push_way(lower, 9, lambda zp: dk1_src.at[block(zp)], dk1_buf.at[own_z])
    dk1_buf[own_z] = dk1_src[own_z]
    dk0_src[...] = dot(ds0[...], q0[...], NN).astype(BF16)
    push_x(8, lambda xp: dk0_src.at[block(xp)], dk0_buf.at[own_x], dk0_buf.at[most_x])
    dk0_buf[own_x] = dk0_src[own_x]
    across(dq1_src, k1, ds1, NX)
    push_x(9, lambda xp: dq1_src.at[block(xp)], dq1_buf.at[own_x], dq1_buf.at[most_x])
    dq1_buf[own_x] = dq1_src[own_x]

    proj = from_y(1)
    mixer_grad = inv * value_grad - mix_buf[...] * (inv * inv * inv * proj / width)
    conv_grad = (mixer_grad * go[...].astype(F32)).astype(BF16).astype(F32)
    sums = []
    for g in range(groups):
        pairs = dot(jnp.where(lane_group == g, conv_grad, 0.0).astype(BF16), win_back[...], NT)
        pairs = pltpu.roll(pairs, 1, 1, stride=1, stride_axis=0)
        sums.append(jnp.sum(pairs[:, taps:], axis=0, keepdims=True))
    fx_buf[x] = jnp.concatenate(sums, axis=0).astype(BF16)
    push_x(10, lambda xp: fx_buf.at[x], fx_buf.at[x], fx_buf.at[pl.ds(0, NX - 1)])
    ggo_o[...] = (mixer_grad * conv_buf[...]).astype(BF16)
    store(ggo_o, ggo_h)
    arrive_x(7, att1_buf.at[most_x])
    att_o[:, head1] = added(att1_buf, NX).T.astype(BF16)
    arrive_way(lower, 7, lambda zp: att0_buf.at[block(zp)])
    att_o[:, head0] = added(att0_buf, NZ).T.astype(BF16)
    store(att_o, att_h)
    arrive_x(10, fx_buf.at[pl.ds(0, NX - 1)])
    total = fx_buf[0].astype(F32)
    for i in range(1, NX):
        total = total + fx_buf[i].astype(F32)
    fz_buf[z] = total.astype(BF16)
    early = list(ends)
    push_z(2, lambda zp: fz_buf.at[z], fz_buf.at[z], fz_buf.at[pl.ds(0, NZ - 1)])

    arrive_x(8, dk0_buf.at[most_x])
    dk_o[:, head0] = (added(dk0_buf, NX) * scale).astype(BF16)
    arrive_way(higher, 9, lambda zp: dk1_buf.at[block(zp)])
    dk_o[:, head1] = (added(dk1_buf, NZ) * scale).astype(BF16)
    store(dk_o, dk_h)
    arrive_x(9, dq1_buf.at[most_x])
    dq_o[:, head1] = (added(dq1_buf, NX).T * scale).astype(BF16)
    arrive_way(lower, 8, lambda zp: dq0_buf.at[block(zp)])
    dq_o[:, head0] = (added(dq0_buf, NZ).T * scale).astype(BF16)
    store(dq_o, dq_h)

    for end in early:
        end()
    for way, finish in one_way:
        way(finish)

    @pl.when(ctx < last)
    def _():
        halo(after).wait_send()

    arrive_z(2, fz_buf.at[pl.ds(0, NZ - 1)])
    total = fz_buf[0].astype(F32)
    for i in range(1, NZ):
        total = total + fz_buf[i].astype(F32)
    gf_o[...] = total
    store(gf_o, gf_h)

    ends[-1]()
    for copy in stores:
        copy.wait()


def write_out(*refs):
    held, sems = refs[10:15], refs[15]
    loads = [pltpu.make_async_copy(refs[i], held[i], sems.at[i]) for i in range(5)]
    stores = [pltpu.make_async_copy(held[i], refs[5 + i], sems.at[5 + i]) for i in range(5)]
    for load in loads:
        load.start()
    for load, store in zip(loads, stores):
        load.wait()
        store.start()
    for store in stores:
        store.wait()


def solution(mesh):
    NZ, NY = mesh.shape["ctx"] // NX, mesh.shape["ch"] // NC

    def on_device(go, gi, ci, filt, q, k, cot):
        rows, chans = go.shape
        groups, taps = filt.shape
        along_x, along_z = NX * rows, NZ * rows
        vmem, sem = pltpu.VMEM, pltpu.SemaphoreType.DMA
        block = jax.ShapeDtypeStruct((rows, chans), BF16)
        outs = [block] * 4 + [jax.ShapeDtypeStruct((groups, taps), F32)]
        own = vmem((rows, chans), BF16)
        row_x, row_z = vmem((along_x, HEAD_DIM), BF16), vmem((along_z, HEAD_DIM), BF16)
        results = pl.pallas_call(
            functools.partial(kernel, NZ, NY),
            out_shape=outs,
            in_specs=[pl.BlockSpec(memory_space=pltpu.HBM)] * 7,
            out_specs=[pl.BlockSpec(memory_space=pltpu.HBM)] * 5,
            scratch_shapes=[
                own, own, own, vmem((groups, taps), BF16),
                vmem((2 * rows, chans), BF16), vmem((2 * rows, chans), BF16), vmem((groups * rows, 2 * taps), BF16),
                vmem((rows, chans), F32), vmem((rows, chans), F32),
                row_x, row_x, row_z, row_z, row_z, row_z, row_x, row_x,
                vmem((NZ, along_x, rows), F32), vmem((NZ, along_x, rows), F32),
                vmem((NZ, rows, along_x), F32), vmem((NZ, rows, along_x), F32),
                vmem((along_x, along_z), BF16), vmem((along_x, along_z), BF16),
                vmem((along_z, along_x), BF16), vmem((along_z, along_x), BF16),
                vmem((NZ, NZ, rows), F32), vmem((NZ, NZ, rows), F32), vmem((NZ, rows), F32), vmem((NZ, rows), F32),
                vmem((NZ, rows), F32), vmem((NZ, along_x), F32), vmem((NZ, along_x), F32), vmem((NX, 8, rows), F32), vmem((NX, 8, rows), F32),
                vmem((2, NC, 8, rows), F32), vmem((2, NY, 8, rows), F32),
                vmem((NX, groups, taps), BF16), vmem((NZ, groups, taps), BF16),
                row_x, row_x, row_z, row_z, row_z, row_z, row_x, row_x,
                row_x, row_x, row_z, row_z, row_z, row_z, row_x, row_x,
                own, own, own, own, vmem((groups, taps), F32),
                sem((10,)), sem((5,)), sem((11,)), sem((11,)), sem((10, NZ)), sem((10, NZ)), sem((3,)), sem((3,)),
                sem((2,)), sem((2,)), sem((2,)), sem((2,)), sem, sem,
            ],
            compiler_params=pltpu.CompilerParams(
                collective_id=0, has_side_effects=True, vmem_limit_bytes=VMEM_GRANT
            ),
            name="hyena",
        )(go, gi, ci, filt, q, k, cot)
        return pl.pallas_call(
            write_out,
            out_shape=outs,
            in_specs=[pl.BlockSpec(memory_space=pltpu.HBM)] * 5,
            out_specs=[pl.BlockSpec(memory_space=pltpu.HBM)] * 5,
            scratch_shapes=[vmem(o.shape, o.dtype) for o in outs] + [sem((10,))],
            compiler_params=pltpu.CompilerParams(vmem_limit_bytes=VMEM_GRANT),
            name="write_out",
        )(*results)

    block = P("ctx", "ch")
    return jax.shard_map(
        on_device,
        mesh=mesh,
        in_specs=(block, block, block, P("ch", None), block, block, block),
        out_specs=(block, block, block, block, P("ch", None)),
        check_vma=False,
    )
```
